256 devices in a mesh: row: 8 (over x, core), col: 2 (over z_lo), chan: 16 (over y, z_hi).
Axes of the slice: x: 4, y: 4, z: 8 (z_hi: 4, z_lo: 2; z = z_hi * 2 + z_lo), core: 2. Of those that a mesh axis runs over, the one named last changes fastest.
Arguments:
- pair: float32 [128, 1024, 1024], P('chan', 'row', 'col'), may hold values from -6 to 6
- pair_mask: int32 [1024, 1024], P('row', 'col'), may hold values 0 or 1
- norm_gain: float32 [128], replicated, may hold values from 0.1 to 1.9
- norm_bias: float32 [128], replicated, may hold values from -3 to 3
- in_weight: bfloat16 [128, 512], replicated, may hold values from -0.5 to 0.5
- gate_weight: bfloat16 [128, 128], replicated, may hold values from -0.5 to 0.5
- hidden_gain: float32 [128], replicated, may hold values from 0.1 to 1.9
- hidden_bias: float32 [128], replicated, may hold values from -3 to 3
- out_weight: bfloat16 [128, 128], replicated, may hold values from -0.5 to 0.5
Outputs:
- update: float32 [128, 1024, 1024], P('chan', 'row', 'col')
The draws below stay inside these ranges and needn't reach their ends.
All inputs are finite; a program needn't handle non-finite values. No bound on the sum of `pair_mask` on one device may be relied on, other than what follows from the above.
Results may differ from the reference program's by a relative error of at most 0.0031.
Values may be sent and summed in bfloat16 or wider, within the bound.
A program may use at most 64 MiB of HBM per device.

```python
import math
import jax
import jax.numpy as jnp
from jax import lax

C = 128
H = 128
N = 1024


def place_ends(values, stream_key, smallest, largest):
    shape = values.shape
    spot = [jax.random.randint(jax.random.fold_in(stream_key, axis), (), 0, shape[axis]) for axis in range(len(shape))]
    values = values.at[tuple(spot)].set(smallest)
    longest = shape.index(max(shape))
    spot[longest] = (spot[longest] + 1) % shape[longest]
    return values.at[tuple(spot)].set(largest)


def steps_of(stream_key, dims, cuts, least, largest):
    factor_of, own = 1.0, jax.random.fold_in(stream_key, 6)
    for position, shards_of in cuts:
        draws = jnp.exp(jax.random.uniform(jax.random.fold_in(own, position), (shards_of,), jnp.float32, least / len(cuts), largest / len(cuts)))
        factor_of = factor_of * jnp.repeat(draws, dims[position] // shards_of).reshape([-1 if axis == position else 1 for axis in range(len(dims))])
    return factor_of


def noise(key, shape, spread, limit, pieces=(), kind=jnp.bfloat16):
    level = steps_of(key, shape, pieces, -0.22, 0.18) if pieces else 1.0
    result = jax.random.normal(key, shape, jnp.float32) * spread * level
    return jnp.minimum(jnp.maximum(result, -limit), limit).astype(kind)


def setup_inputs(seed: int = 0) -> dict:
    splits = jax.random.split(jax.random.key(seed), 10)
    return {
        "pair": noise(splits[0], (C, N, N), 1.0, 6.0, ((0, 16), (1, 8), (2, 2)), jnp.float32),
        "pair_mask": place_ends((jax.random.randint(splits[1], (N, N), 0, 8) < 7).astype(jnp.int32), jax.random.fold_in(splits[1], 1), 0, 1),
        "norm_gain": jnp.clip(1.0 + 0.18 * jax.random.normal(splits[2], (C,), jnp.float32), 0.1, 1.9),
        "norm_bias": noise(splits[3], (C,), 0.5, 3.0, (), jnp.float32),
        "in_weight": noise(splits[4], (C, 4 * H), C ** -0.5, 0.5),
        "gate_weight": noise(splits[5], (C, C), C ** -0.5, 0.5),
        "hidden_gain": jnp.clip(1.0 + 0.18 * jax.random.normal(splits[6], (H,), jnp.float32), 0.1, 1.9),
        "hidden_bias": noise(splits[7], (H,), 0.5, 3.0, (), jnp.float32),
        "out_weight": noise(splits[8], (H, C), H ** -0.5, 0.5),
    }


EPS = 1e-05

def layer_norm(values, gain, bias):
    mean = lax.optimization_barrier(jnp.mean(values, axis=0, keepdims=True))
    centred = values - mean
    var = lax.optimization_barrier(jnp.mean(centred * centred, axis=0, keepdims=True))
    return centred * lax.rsqrt(var + EPS) * gain[:, None, None] + bias[:, None, None]

def reference(pair, pair_mask, norm_gain, norm_bias, in_weight, gate_weight, hidden_gain, hidden_bias, out_weight):
    block = math.gcd(N, 64)
    starts = jnp.arange(N // block, dtype=jnp.int32) * block

    def project(start):
        rows = lax.dynamic_slice_in_dim(pair, start, block, 1)
        normed = layer_norm(rows, norm_gain, norm_bias).astype(jnp.bfloat16)
        mask_rows = lax.dynamic_slice_in_dim(pair_mask, start, block, 0).astype(jnp.float32)
        proj = jnp.einsum('cij,cf->fij', normed.astype(jnp.float32), in_weight.astype(jnp.float32))
        left = (jax.nn.sigmoid(proj[:H]) * proj[H:2 * H] * mask_rows).astype(jnp.bfloat16)
        right = (jax.nn.sigmoid(proj[2 * H:3 * H]) * proj[3 * H:] * mask_rows).astype(jnp.bfloat16)
        gate = jax.nn.sigmoid(jnp.einsum('eij,ec->cij', normed.astype(jnp.float32), gate_weight.astype(jnp.float32)))
        return (left, right, gate)
    left_b, right_b, gate_b = lax.map(project, starts)
    left = jnp.moveaxis(left_b, 0, 1).reshape(H, N, N)
    right = jnp.moveaxis(right_b, 0, 1).reshape(H, N, N)
    gate = jnp.moveaxis(gate_b, 0, 1).reshape(C, N, N)

    def contract(pairs):
        return jnp.einsum('hik,hjk->hij', pairs[0].astype(jnp.float32), pairs[1].astype(jnp.float32))
    hidden = lax.map(contract, (left.reshape(H // 8, 8, N, N), right.reshape(H // 8, 8, N, N))).reshape(H, N, N)
    hnorm = layer_norm(hidden, hidden_gain, hidden_bias).astype(jnp.bfloat16)
    projected = jnp.einsum('hij,hc->cij', hnorm.astype(jnp.float32), out_weight.astype(jnp.float32))
    return gate * projected
```

```python
import jax
import jax.numpy as jnp
from jax import lax
from jax.sharding import PartitionSpec as P

EPS = 1e-05
AXES = ("row", "col", "chan")
STEP = 6.0 / 32767.0


def shards(
    pair,
    pair_mask,
    norm_gain,
    norm_bias,
    in_weight,
    gate_weight,
    hidden_gain,
    hidden_bias,
    out_weight,
):
    hid = 128
    chan = lax.axis_index("chan")
    row = lax.axis_index("row")
    fixed = jnp.round(pair * (1.0 / STEP)).astype(jnp.int16)
    blocks = fixed.reshape(8, 4, 32, 4, 128).transpose(1, 3, 0, 2, 4).reshape(16, 8, 32, 128)
    grouped = lax.all_to_all(blocks, "chan", split_axis=0, concat_axis=0, tiled=True)
    values = grouped.reshape(128, 4096).astype(jnp.float32) * STEP
    mask = lax.dynamic_slice(pair_mask, ((chan // 4) * 32, (chan % 4) * 128), (32, 128))
    mask = mask.reshape(4096).astype(jnp.float32)
    mean = jnp.mean(values, axis=0, keepdims=True)
    centred = values - mean
    var = jnp.mean(centred * centred, axis=0, keepdims=True)
    normed = centred * lax.rsqrt(var + EPS) * norm_gain[:, None] + norm_bias[:, None]
    normed = normed.astype(jnp.bfloat16)
    proj = jnp.einsum("cp,cf->fp", normed, in_weight, preferred_element_type=jnp.float32)
    left = (jax.nn.sigmoid(proj[:hid]) * proj[hid : 2 * hid] * mask).astype(jnp.bfloat16)
    right = (jax.nn.sigmoid(proj[2 * hid : 3 * hid]) * proj[3 * hid :] * mask).astype(jnp.bfloat16)
    both = jnp.stack([left.reshape(4, 32, 2, 16, 128), right.reshape(4, 32, 2, 16, 128)], axis=3)
    both = both.transpose(0, 2, 1, 3, 4, 5).reshape(256, 2, 16, 128)
    both = lax.all_to_all(both, AXES, split_axis=0, concat_axis=0, tiled=True)
    both = both.reshape(8, 2, 4, 4, 2, 16, 128).transpose(4, 0, 2, 5, 1, 3, 6).reshape(2, 512, 1024)
    own = both[1].reshape(32, 16, 1024)
    other = lax.ppermute(both[1], "row", [(r, r ^ 1) for r in range(8)]).reshape(32, 16, 1024)
    odd = row % 2 == 1
    full = jnp.stack([jnp.where(odd, other, own), jnp.where(odd, own, other)], axis=1)
    full = full.reshape(1024, 1024)
    hidden = jnp.einsum("ik,jk->ij", both[0], full, preferred_element_type=jnp.float32)
    hidden = hidden.astype(jnp.bfloat16)
    hidden = hidden.reshape(8, 4, 16, 2, 4, 128).transpose(0, 3, 1, 4, 2, 5).reshape(256, 16, 128)
    hidden = lax.all_to_all(hidden, AXES, split_axis=0, concat_axis=0, tiled=True)
    hidden = hidden.reshape(4, 2, 32, 16, 128).transpose(0, 2, 1, 3, 4).reshape(128, 4096)
    wide = hidden.astype(jnp.float32)
    nu = jnp.mean(wide, axis=0, keepdims=True)
    dev = wide - nu
    tau = jnp.mean(dev * dev, axis=0, keepdims=True)
    scaled = hidden_gain[:, None] * out_weight.astype(jnp.float32)
    high = lax.reduce_precision(scaled, 8, 7)
    low = lax.reduce_precision(scaled - high, 8, 7)
    pieces = jnp.concatenate([high, low], axis=0).astype(jnp.bfloat16)
    raw = jnp.einsum(
        "hp,hc->cp",
        jnp.concatenate([hidden, hidden], axis=0),
        pieces,
        preferred_element_type=jnp.float32,
    )
    column = jnp.sum(high + low, axis=0)
    offset = jnp.sum(hidden_bias[:, None] * out_weight.astype(jnp.float32), axis=0)
    projected = (raw - nu * column[:, None]) * lax.rsqrt(tau + EPS) + offset[:, None]
    gate = jax.nn.sigmoid(
        jnp.einsum("ep,ec->cp", normed, gate_weight, preferred_element_type=jnp.float32)
    )
    update = (gate * projected).astype(jnp.bfloat16).reshape(16, 8, 32, 128)
    owned = lax.all_to_all(update, "chan", split_axis=0, concat_axis=0, tiled=True)
    owned = owned.reshape(4, 4, 8, 32, 128).transpose(2, 0, 3, 1, 4).reshape(8, 128, 512)
    return owned.astype(jnp.float32)


def solution(mesh):
    placed = (P("chan", "row", "col"), P("row", "col"), P(), P(), P(), P(), P(), P(), P())
    return jax.shard_map(
        shards, mesh=mesh, in_specs=placed, out_specs=P("chan", "row", "col"), check_vma=False
    )
```

```python
import jax
import jax.numpy as jnp
from jax import lax
from jax.experimental import pallas as pl
from jax.experimental.pallas import tpu as pltpu
from jax.sharding import PartitionSpec as P

EPS = 1e-05
MESH = pl.DeviceIdType.MESH
STEP = 6.0 / 32767.0
R0, R1, L0, L1 = range(4)


def kernel(
    pair,
    mask,
    norm_gain,
    norm_bias,
    in_weight,
    gate_weight,
    hidden_gain,
    hidden_bias,
    out_weight,
    out,
    enc,
    got,
    flat,
    flat2,
    maskf,
    columns,
    wt,
    pieces,
    sides,
    across,
    rights,
    lefts,
    product,
    plane,
    hidden,
    gate,
    upd,
    owned,
    enc_send,
    enc_recv,
    side_send,
    side_recv,
    plane_send,
    right_recv,
    left_recv,
    twin_send,
    twin_recv,
    prod_send,
    prod_recv,
    hid_send,
    hid_recv,
    upd_send,
    upd_recv,
):
    row, col, chan = lax.axis_index("row"), lax.axis_index("col"), lax.axis_index("chan")
    x, core = row // 2, lax.rem(row, 2)
    y, zhi = chan // 4, lax.rem(chan, 4)
    z = zhi * 2 + col

    def at(r, c, h):
        return {"row": r, "col": c, "chan": h}

    def wait(ref, sem):
        pltpu.make_async_copy(ref, ref, sem).wait()

    def remote(src, dst, send, recv, device):
        pltpu.make_async_remote_copy(
            src_ref=src,
            dst_ref=dst,
            send_sem=send,
            recv_sem=recv,
            device_id=device,
            device_id_type=MESH,
        ).start()

    def block_of(zz):
        return pl.ds(pl.multiple_of((lax.rem(zz, 2) * 4 + zz // 2) * 128, 128), 128)

    barrier = pltpu.get_barrier_semaphore()

    def greet(device):
        pl.semaphore_signal(barrier, inc=1, device_id=device, device_id_type=MESH)

    def greet_chan(t, carry):
        greet(at(row, col, lax.rem(chan + t, 16)))
        return carry

    def greet_z(t, carry):
        greet(at(row, 1 - col, y * 4 + t))
        return carry

    def greet_plane(t, carry):
        greet(at(lax.rem(row + 1 + t // 4, 8), col, lax.rem(t, 4) * 4 + zhi))
        return carry

    lax.fori_loop(1, 16, greet_chan, 0)
    lax.fori_loop(0, 4, greet_z, 0)
    lax.fori_loop(0, 28, greet_plane, 0)

    def encode(q):
        for p in range(16):
            part = pair[:, (p // 4) * 32 + q * 16 :, (p % 4) * 128 :][:, :16, :128]
            enc[q, p] = jnp.round(part * (1.0 / STEP)).astype(jnp.int32).astype(jnp.int16)

    def send_enc(q):
        mine = pl.ds(pl.multiple_of(chan * 8, 8), 8)

        def go(t, carry):
            p = lax.rem(chan + t, 16)
            remote(
                enc.at[q, p], got.at[q, mine], enc_send.at[q], enc_recv.at[q], at(row, col, p)
            )
            return carry

        lax.fori_loop(1, 16, go, 0)
        pltpu.make_async_copy(enc.at[q, chan], got.at[q, mine], enc_recv.at[q]).start()

    encode(0)
    pl.semaphore_wait(barrier, 47)
    send_enc(0)
    encode(1)
    send_enc(1)

    wt[:512] = in_weight[...].astype(jnp.float32).T.astype(jnp.bfloat16)
    wt[512:] = gate_weight[...].astype(jnp.float32).T.astype(jnp.bfloat16)
    columns[0] = jnp.broadcast_to(norm_gain[...], (128, 128)).T
    columns[1] = jnp.broadcast_to(norm_bias[...], (128, 128)).T
    out_t = out_weight[...].astype(jnp.float32).T
    scaled = out_t * hidden_gain[...]
    high = scaled.astype(jnp.bfloat16)
    low = (scaled - high.astype(jnp.float32)).astype(jnp.bfloat16)
    pieces[:, :128] = high
    pieces[:, 128:] = low
    total = jnp.sum(high.astype(jnp.float32) + low.astype(jnp.float32), axis=1, keepdims=True)
    columns[2] = jnp.broadcast_to(total, (128, 128))
    offset = jnp.sum(out_t * hidden_bias[...], axis=1, keepdims=True)
    columns[3] = jnp.broadcast_to(offset, (128, 128))
    rows_mine = pl.ds(pl.multiple_of(y * 32, 32), 32)
    maskf[...] = mask[rows_mine, pl.ds(pl.multiple_of(zhi * 128, 128), 128)].astype(jnp.float32)

    def twice(a):
        return jnp.concatenate([a, a], axis=1)

    def rows_of(ref, i):
        return jnp.concatenate(
            [ref[pl.ds(2 * i, 128, stride=16), :], ref[pl.ds(2 * i + 1, 128, stride=16), :]],
            axis=1,
        )

    def put_rows(ref, i, value):
        ref[pl.ds(2 * i, 128, stride=16), :] = value[:, :128]
        ref[pl.ds(2 * i + 1, 128, stride=16), :] = value[:, 128:]

    def project(q):
        flat[...] = got[q].astype(jnp.int32).astype(jnp.float32).reshape(2048, 128) * STEP

        def step(i, carry):
            value = rows_of(flat, i)
            mean = jnp.sum(value, axis=0, keepdims=True) * (1.0 / 128)
            centred = value - mean
            var = jnp.sum(centred * centred, axis=0, keepdims=True) * (1.0 / 128)
            normed = centred * lax.rsqrt(var + EPS) * twice(columns[0]) + twice(columns[1])
            normed = normed.astype(jnp.bfloat16)
            present = jnp.concatenate(
                [
                    maskf[pl.ds(q * 16 + 2 * i, 1), :],
                    maskf[pl.ds(q * 16 + 2 * i + 1, 1), :],
                ],
                axis=1,
            )

            def proj(k):
                return jnp.dot(
                    wt[k * 128 : k * 128 + 128, :], normed, preferred_element_type=jnp.float32
                )

            put_rows(flat, i, jax.nn.sigmoid(proj(0)) * proj(1) * present)
            put_rows(flat2, i, jax.nn.sigmoid(proj(2)) * proj(3) * present)
            gated = jax.nn.sigmoid(proj(4))
            gate[q, 2 * i] = gated[:, :128]
            gate[q, 2 * i + 1] = gated[:, 128:]
            return carry

        lax.fori_loop(0, 8, step, 0)
        sides[L0 + q] = flat[...].reshape(128, 16, 128).astype(jnp.bfloat16)
        sides[R0 + q] = flat2[...].reshape(128, 16, 128).astype(jnp.bfloat16)

    def send_sides(s):
        def go(t, carry):
            zz = lax.rem(z + t, 8)
            remote(
                sides.at[s, pl.ds(pl.multiple_of(zz * 16, 16), 16)],
                across.at[s, :, :, block_of(z)],
                side_send.at[s],
                side_recv.at[s],
                at(row, lax.rem(zz, 2), y * 4 + zz // 2),
            )
            return carry

        lax.fori_loop(1, 8, go, 0)
        pltpu.make_async_copy(
            sides.at[s, pl.ds(pl.multiple_of(z * 16, 16), 16)],
            across.at[s, :, :, block_of(z)],
            side_recv.at[s],
        ).start()

    def send_plane(s):
        q = s % 2
        ours = pl.ds(pl.multiple_of((row * 4 + y) * 16, 16), 16)
        dst = rights.at[q, ours] if s < L0 else lefts.at[ours]
        recv = right_recv if s < L0 else left_recv
        wait(across.at[s], side_recv.at[s])

        def go(t, carry):
            k = lax.rem(x * 4 + y + t, 16)
            remote(
                across.at[s, k],
                dst,
                plane_send.at[s],
                recv,
                at((k // 4) * 2 + q, col, lax.rem(k, 4) * 4 + zhi),
            )
            return carry

        lax.fori_loop(1, 16, go, 0)

        @pl.when(core == q)
        def _():
            pltpu.make_async_copy(across.at[s, x * 4 + y], dst, recv).start()

        @pl.when(core != q)
        def _():
            go(0, 0)

    wait(got.at[0], enc_recv.at[0])
    project(0)
    send_sides(R0)
    wait(got.at[1], enc_recv.at[1])
    project(1)
    send_sides(R1)
    send_sides(L0)
    send_sides(L1)
    send_plane(R0)
    send_plane(R1)

    wait(rights.at[core], right_recv)
    remote(rights.at[core], rights.at[core], twin_send, twin_recv, at(x * 2 + 1 - core, col, chan))
    send_plane(L0)

    def multiply():
        wait(rights.at[1 - core], twin_recv)
        wait(lefts, left_recv)

        def step(n, carry):
            parts = []
            for m in range(2):
                for yy in range(4):
                    for q in range(2):
                        start = pl.multiple_of((n * 2 + m) * 64 + yy * 16, 16)
                        parts.append(rights[q, pl.ds(start, 16), :])
            block = jnp.concatenate(parts, axis=0)
            result = lax.dot_general(
                lefts[...], block, (((1,), (1,)), ((), ())), preferred_element_type=jnp.float32
            )
            product[:, pl.ds(pl.multiple_of(n * 256, 256), 256)] = result.astype(jnp.bfloat16)
            return carry

        lax.fori_loop(0, 4, step, 0)

        def go(t, carry):
            k = lax.rem(row * 4 + y + t, 32)
            remote(
                product.at[pl.ds(pl.multiple_of(k * 16, 16), 16)],
                plane.at[core, x * 4 + y],
                prod_send,
                prod_recv.at[core],
                at(k // 4, col, lax.rem(k, 4) * 4 + zhi),
            )
            return carry

        lax.fori_loop(1, 32, go, 0)
        pltpu.make_async_copy(
            product.at[pl.ds(pl.multiple_of((row * 4 + y) * 16, 16), 16)],
            plane.at[core, x * 4 + y],
            prod_recv.at[core],
        ).start()

    def send_hidden(q):
        wait(plane.at[q], prod_recv.at[q])
        dst = hidden.at[q, pl.ds(pl.multiple_of(z * 16, 16), 16)]

        def go(t, carry):
            zz = lax.rem(z + t, 8)
            remote(
                plane.at[q, :, :, block_of(zz)],
                dst,
                hid_send.at[q],
                hid_recv.at[q],
                at(row, lax.rem(zz, 2), y * 4 + zz // 2),
            )
            return carry

        lax.fori_loop(1, 8, go, 0)
        pltpu.make_async_copy(plane.at[q, :, :, block_of(z)], dst, hid_recv.at[q]).start()

    @pl.when(core == 0)
    def _():
        multiply()

    send_plane(L1)
    send_hidden(0)

    @pl.when(core == 1)
    def _():
        multiply()

    send_hidden(1)

    def finish(q):
        wait(hidden.at[q], hid_recv.at[q])
        flat[...] = hidden[q].astype(jnp.float32).reshape(2048, 128)

        def step(i, carry):
            value = rows_of(flat, i)
            nu = jnp.sum(value, axis=0, keepdims=True) * (1.0 / 128)
            dev = value - nu
            tau = jnp.sum(dev * dev, axis=0, keepdims=True) * (1.0 / 128)
            short = value.astype(jnp.bfloat16)
            raw = jnp.dot(
                pieces[...],
                jnp.concatenate([short, short], axis=0),
                preferred_element_type=jnp.float32,
            )
            out_rows = (raw - twice(columns[2]) * nu) * lax.rsqrt(tau + EPS) + twice(columns[3])
            gated = jnp.concatenate([gate[q, 2 * i], gate[q, 2 * i + 1]], axis=1)
            put_rows(flat2, i, gated * out_rows)
            return carry

        lax.fori_loop(0, 8, step, 0)
        upd[q] = flat2[...].reshape(128, 16, 128).astype(jnp.bfloat16)
        dst = owned.at[
            :,
            pl.ds(pl.multiple_of(y * 32 + q * 16, 16), 16),
            pl.ds(pl.multiple_of(zhi * 128, 128), 128),
        ]

        def go(t, carry):
            p = lax.rem(chan + t, 16)
            remote(
                upd.at[q, pl.ds(pl.multiple_of(p * 8, 8), 8)],
                dst,
                upd_send.at[q],
                upd_recv,
                at(row, col, p),
            )
            return carry

        lax.fori_loop(1, 16, go, 0)
        pltpu.make_async_copy(
            upd.at[q, pl.ds(pl.multiple_of(chan * 8, 8), 8)], dst, upd_recv
        ).start()

    finish(0)
    finish(1)

    for q in range(2):
        wait(enc.at[q, :15], enc_send.at[q])
        wait(plane.at[q, :14], hid_send.at[q])
        wait(upd.at[q, :120], upd_send.at[q])
    for s in range(4):
        wait(sides.at[s, :112], side_send.at[s])

        @pl.when(core == s % 2)
        def _():
            wait(across.at[s, :15], plane_send.at[s])

        @pl.when(core != s % 2)
        def _():
            wait(across.at[s], plane_send.at[s])

    wait(rights.at[core], twin_send)
    wait(product.at[: 31 * 16], prod_send)
    wait(owned, upd_recv)
    out[...] = owned[...]


def shards(
    pair,
    pair_mask,
    norm_gain,
    norm_bias,
    in_weight,
    gate_weight,
    hidden_gain,
    hidden_bias,
    out_weight,
):
    bf16, f32 = jnp.bfloat16, jnp.float32
    dma = pltpu.SemaphoreType.DMA
    vmem = pl.BlockSpec(memory_space=pltpu.VMEM)
    update = pl.pallas_call(
        kernel,
        out_shape=jax.ShapeDtypeStruct((8, 128, 512), bf16),
        in_specs=[vmem] * 9,
        out_specs=vmem,
        scratch_shapes=[
            pltpu.VMEM((2, 16, 8, 16, 128), jnp.int16),
            pltpu.VMEM((2, 128, 16, 128), jnp.int16),
            pltpu.VMEM((2048, 128), f32),
            pltpu.VMEM((2048, 128), f32),
            pltpu.VMEM((32, 128), f32),
            pltpu.VMEM((4, 128, 128), f32),
            pltpu.VMEM((640, 128), bf16),
            pltpu.VMEM((128, 256), bf16),
            pltpu.VMEM((4, 128, 16, 128), bf16),
            pltpu.VMEM((4, 16, 16, 1024), bf16),
            pltpu.VMEM((2, 512, 1024), bf16),
            pltpu.VMEM((512, 1024), bf16),
            pltpu.VMEM((512, 1024), bf16),
            pltpu.VMEM((2, 16, 16, 1024), bf16),
            pltpu.VMEM((2, 128, 16, 128), bf16),
            pltpu.VMEM((2, 16, 128, 128), f32),
            pltpu.VMEM((2, 128, 16, 128), bf16),
            pltpu.VMEM((8, 128, 512), bf16),
            dma((2,)),
            dma((2,)),
            dma((4,)),
            dma((4,)),
            dma((4,)),
            dma,
            dma,
            dma,
            dma,
            dma,
            dma((2,)),
            dma((2,)),
            dma((2,)),
            dma((2,)),
            dma,
        ],
        compiler_params=pltpu.CompilerParams(
            collective_id=0, has_side_effects=True, vmem_limit_bytes=48 * 2**20
        ),
        name="triangle",
    )(
        pair,
        pair_mask,
        norm_gain.reshape(1, 128),
        norm_bias.reshape(1, 128),
        in_weight,
        gate_weight,
        hidden_gain.reshape(1, 128),
        hidden_bias.reshape(1, 128),
        out_weight,
    )
    return update.astype(f32)


def solution(mesh):
    placed = (P("chan", "row", "col"), P("row", "col"), P(), P(), P(), P(), P(), P(), P())
    return jax.shard_map(
        shards, mesh=mesh, in_specs=placed, out_specs=P("chan", "row", "col"), check_vma=False
    )
```

```python
import jax
import jax.numpy as jnp
from jax import lax
from jax.experimental import pallas as pl
from jax.experimental.pallas import tpu as pltpu
from jax.sharding import PartitionSpec as P

EPS = 1e-05
MESH = pl.DeviceIdType.MESH
STEP = 6.0 / 32767.0
R0, R1, L0, L1 = range(4)


def kernel(
    pair_in,
    mask_in,
    norm_gain_in,
    norm_bias_in,
    in_weight_in,
    gate_weight_in,
    hidden_gain_in,
    hidden_bias_in,
    out_weight_in,
    out,
    pair,
    mask,
    norm_gain,
    norm_bias,
    in_weight,
    gate_weight,
    hidden_gain,
    hidden_bias,
    out_weight,
    enc,
    got,
    flat,
    flat2,
    maskf,
    columns,
    wt,
    pieces,
    sides,
    across,
    rights,
    lefts,
    product,
    plane,
    hidden,
    gate,
    upd,
    owned,
    pair_sem,
    load_sem,
    enc_send,
    enc_recv,
    side_send,
    side_recv,
    plane_send,
    right_recv,
    left_recv,
    twin_send,
    twin_recv,
    prod_send,
    prod_recv,
    hid_send,
    hid_recv,
    upd_send,
    upd_recv,
):
    row, col, chan = lax.axis_index("row"), lax.axis_index("col"), lax.axis_index("chan")
    x, core = row // 2, lax.rem(row, 2)
    y, zhi = chan // 4, lax.rem(chan, 4)
    z = zhi * 2 + col

    def at(r, c, h):
        return {"row": r, "col": c, "chan": h}

    def wait(ref, sem):
        pltpu.make_async_copy(ref, ref, sem).wait()

    def remote(src, dst, send, recv, device):
        pltpu.make_async_remote_copy(
            src_ref=src,
            dst_ref=dst,
            send_sem=send,
            recv_sem=recv,
            device_id=device,
            device_id_type=MESH,
        ).start()

    def block_of(zz):
        return pl.ds(pl.multiple_of((lax.rem(zz, 2) * 4 + zz // 2) * 128, 128), 128)

    for q in range(2):
        for k in range(4):
            pltpu.make_async_copy(
                pair_in.at[:, k * 32 + q * 16 : k * 32 + q * 16 + 16], pair.at[q, k], pair_sem.at[q]
            ).start()
    rows_mine = pl.ds(pl.multiple_of(y * 32, 32), 32)
    loads = [
        pltpu.make_async_copy(src, dst, load_sem.at[n])
        for n, (src, dst) in enumerate(
            [
                (mask_in.at[rows_mine, pl.ds(pl.multiple_of(zhi * 128, 128), 128)], mask),
                (norm_gain_in, norm_gain),
                (norm_bias_in, norm_bias),
                (in_weight_in, in_weight),
                (gate_weight_in, gate_weight),
                (hidden_gain_in, hidden_gain),
                (hidden_bias_in, hidden_bias),
                (out_weight_in, out_weight),
            ]
        )
    ]
    for load in loads:
        load.start()

    barrier = pltpu.get_barrier_semaphore()

    def greet(device):
        pl.semaphore_signal(barrier, inc=1, device_id=device, device_id_type=MESH)

    def greet_chan(t, carry):
        greet(at(row, col, lax.rem(chan + t, 16)))
        return carry

    def greet_z(t, carry):
        greet(at(row, 1 - col, y * 4 + t))
        return carry

    def greet_plane(t, carry):
        greet(at(lax.rem(row + 1 + t // 4, 8), col, lax.rem(t, 4) * 4 + zhi))
        return carry

    lax.fori_loop(1, 16, greet_chan, 0)
    lax.fori_loop(0, 4, greet_z, 0)
    lax.fori_loop(0, 28, greet_plane, 0)

    def encode(q):
        wait(pair.at[q], pair_sem.at[q])
        for p in range(16):
            part = pair[q, p // 4, :, :, (p % 4) * 128 : (p % 4) * 128 + 128]
            enc[q, p] = jnp.round(part * (1.0 / STEP)).astype(jnp.int32).astype(jnp.int16)

    def send_enc(q):
        mine = pl.ds(pl.multiple_of(chan * 8, 8), 8)

        def go(t, carry):
            p = lax.rem(chan + t, 16)
            remote(
                enc.at[q, p], got.at[q, mine], enc_send.at[q], enc_recv.at[q], at(row, col, p)
            )
            return carry

        lax.fori_loop(1, 16, go, 0)
        pltpu.make_async_copy(enc.at[q, chan], got.at[q, mine], enc_recv.at[q]).start()

    encode(0)
    pl.semaphore_wait(barrier, 47)
    send_enc(0)
    encode(1)
    send_enc(1)

    for load in loads:
        load.wait()
    wt[:512] = in_weight[...].astype(jnp.float32).T.astype(jnp.bfloat16)
    wt[512:] = gate_weight[...].astype(jnp.float32).T.astype(jnp.bfloat16)
    columns[0] = jnp.broadcast_to(norm_gain[...], (128, 128)).T
    columns[1] = jnp.broadcast_to(norm_bias[...], (128, 128)).T
    out_t = out_weight[...].astype(jnp.float32).T
    scaled = out_t * hidden_gain[...]
    high = scaled.astype(jnp.bfloat16)
    low = (scaled - high.astype(jnp.float32)).astype(jnp.bfloat16)
    pieces[:, :128] = high
    pieces[:, 128:] = low
    total = jnp.sum(high.astype(jnp.float32) + low.astype(jnp.float32), axis=1, keepdims=True)
    columns[2] = jnp.broadcast_to(total, (128, 128))
    offset = jnp.sum(out_t * hidden_bias[...], axis=1, keepdims=True)
    columns[3] = jnp.broadcast_to(offset, (128, 128))
    maskf[...] = mask[...].astype(jnp.float32)

    def twice(a):
        return jnp.concatenate([a, a], axis=1)

    def rows_of(ref, i):
        return jnp.concatenate(
            [ref[pl.ds(2 * i, 128, stride=16), :], ref[pl.ds(2 * i + 1, 128, stride=16), :]],
            axis=1,
        )

    def put_rows(ref, i, value):
        ref[pl.ds(2 * i, 128, stride=16), :] = value[:, :128]
        ref[pl.ds(2 * i + 1, 128, stride=16), :] = value[:, 128:]

    def project(q):
        flat[...] = got[q].astype(jnp.int32).astype(jnp.float32).reshape(2048, 128) * STEP

        def step(i, carry):
            value = rows_of(flat, i)
            mean = jnp.sum(value, axis=0, keepdims=True) * (1.0 / 128)
            centred = value - mean
            var = jnp.sum(centred * centred, axis=0, keepdims=True) * (1.0 / 128)
            normed = centred * lax.rsqrt(var + EPS) * twice(columns[0]) + twice(columns[1])
            normed = normed.astype(jnp.bfloat16)
            present = jnp.concatenate(
                [
                    maskf[pl.ds(q * 16 + 2 * i, 1), :],
                    maskf[pl.ds(q * 16 + 2 * i + 1, 1), :],
                ],
                axis=1,
            )

            def proj(k):
                return jnp.dot(
                    wt[k * 128 : k * 128 + 128, :], normed, preferred_element_type=jnp.float32
                )

            put_rows(flat, i, jax.nn.sigmoid(proj(0)) * proj(1) * present)
            put_rows(flat2, i, jax.nn.sigmoid(proj(2)) * proj(3) * present)
            gated = jax.nn.sigmoid(proj(4))
            gate[q, 2 * i] = gated[:, :128]
            gate[q, 2 * i + 1] = gated[:, 128:]
            return carry

        lax.fori_loop(0, 8, step, 0)
        sides[L0 + q] = flat[...].reshape(128, 16, 128).astype(jnp.bfloat16)
        sides[R0 + q] = flat2[...].reshape(128, 16, 128).astype(jnp.bfloat16)

    def send_sides(s):
        def go(t, carry):
            zz = lax.rem(z + lax.select(lax.rem(t, 2) == 1, (9 - t) // 2, 4 + t // 2), 8)
            remote(
                sides.at[s, pl.ds(pl.multiple_of(zz * 16, 16), 16)],
                across.at[s, :, :, block_of(z)],
                side_send.at[s],
                side_recv.at[s],
                at(row, lax.rem(zz, 2), y * 4 + zz // 2),
            )
            return carry

        lax.fori_loop(1, 8, go, 0)
        pltpu.make_async_copy(
            sides.at[s, pl.ds(pl.multiple_of(z * 16, 16), 16)],
            across.at[s, :, :, block_of(z)],
            side_recv.at[s],
        ).start()

    def send_plane(s):
        q = s % 2
        ours = pl.ds(pl.multiple_of((row * 4 + y) * 16, 16), 16)
        dst = rights.at[q, ours] if s < L0 else lefts.at[ours]
        recv = right_recv if s < L0 else left_recv
        wait(across.at[s], side_recv.at[s])

        def go(t, carry):
            k = lax.rem(x * 4 + y + t, 16)
            remote(
                across.at[s, k],
                dst,
                plane_send.at[s],
                recv,
                at((k // 4) * 2 + q, col, lax.rem(k, 4) * 4 + zhi),
            )
            return carry

        lax.fori_loop(1, 16, go, 0)

        @pl.when(core == q)
        def _():
            pltpu.make_async_copy(across.at[s, x * 4 + y], dst, recv).start()

        @pl.when(core != q)
        def _():
            go(0, 0)

    def sent(s):
        wait(sides.at[s, :112], side_send.at[s])

    wait(got.at[0], enc_recv.at[0])
    project(0)
    send_sides(R0)
    wait(got.at[1], enc_recv.at[1])
    project(1)
    send_sides(R1)
    sent(R0)
    send_sides(L0)
    send_plane(R0)
    sent(R1)
    send_sides(L1)
    send_plane(R1)

    wait(rights.at[core], right_recv)
    remote(rights.at[core], rights.at[core], twin_send, twin_recv, at(x * 2 + 1 - core, col, chan))
    send_plane(L0)

    def multiply():
        wait(rights.at[1 - core], twin_recv)
        wait(lefts, left_recv)

        def step(n, carry):
            parts = []
            for m in range(2):
                for yy in range(4):
                    for q in range(2):
                        start = pl.multiple_of((n * 2 + m) * 64 + yy * 16, 16)
                        parts.append(rights[q, pl.ds(start, 16), :])
            block = jnp.concatenate(parts, axis=0)
            result = lax.dot_general(
                lefts[...], block, (((1,), (1,)), ((), ())), preferred_element_type=jnp.float32
            )
            product[:, pl.ds(pl.multiple_of(n * 256, 256), 256)] = result.astype(jnp.bfloat16)
            return carry

        lax.fori_loop(0, 4, step, 0)

        def go(t, carry):
            k = lax.rem(row * 4 + y + t, 32)
            remote(
                product.at[pl.ds(pl.multiple_of(k * 16, 16), 16)],
                plane.at[core, x * 4 + y],
                prod_send,
                prod_recv.at[core],
                at(k // 4, col, lax.rem(k, 4) * 4 + zhi),
            )
            return carry

        lax.fori_loop(1, 32, go, 0)
        pltpu.make_async_copy(
            product.at[pl.ds(pl.multiple_of((row * 4 + y) * 16, 16), 16)],
            plane.at[core, x * 4 + y],
            prod_recv.at[core],
        ).start()

    def send_hidden(q):
        wait(plane.at[q], prod_recv.at[q])
        dst = hidden.at[q, pl.ds(pl.multiple_of(z * 16, 16), 16)]

        def go(t, carry):
            zz = lax.rem(z + lax.select(lax.rem(t, 2) == 1, (9 - t) // 2, 4 + t // 2), 8)
            remote(
                plane.at[q, :, :, block_of(zz)],
                dst,
                hid_send.at[q],
                hid_recv.at[q],
                at(row, lax.rem(zz, 2), y * 4 + zz // 2),
            )
            return carry

        lax.fori_loop(1, 8, go, 0)
        pltpu.make_async_copy(plane.at[q, :, :, block_of(z)], dst, hid_recv.at[q]).start()

    @pl.when(core == 0)
    def _():
        multiply()

    send_plane(L1)
    send_hidden(0)

    @pl.when(core == 1)
    def _():
        multiply()

    send_hidden(1)

    def finish(q):
        wait(hidden.at[q], hid_recv.at[q])
        flat[...] = hidden[q].astype(jnp.float32).reshape(2048, 128)

        def step(i, carry):
            value = rows_of(flat, i)
            nu = jnp.sum(value, axis=0, keepdims=True) * (1.0 / 128)
            dev = value - nu
            tau = jnp.sum(dev * dev, axis=0, keepdims=True) * (1.0 / 128)
            short = value.astype(jnp.bfloat16)
            raw = jnp.dot(
                pieces[...],
                jnp.concatenate([short, short], axis=0),
                preferred_element_type=jnp.float32,
            )
            out_rows = (raw - twice(columns[2]) * nu) * lax.rsqrt(tau + EPS) + twice(columns[3])
            gated = jnp.concatenate([gate[q, 2 * i], gate[q, 2 * i + 1]], axis=1)
            put_rows(flat2, i, gated * out_rows)
            return carry

        lax.fori_loop(0, 8, step, 0)
        upd[q] = flat2[...].reshape(128, 16, 128).astype(jnp.bfloat16)
        dst = owned.at[
            :,
            pl.ds(pl.multiple_of(y * 32 + q * 16, 16), 16),
            pl.ds(pl.multiple_of(zhi * 128, 128), 128),
        ]

        def go(t, carry):
            p = lax.rem(chan + t, 16)
            remote(
                upd.at[q, pl.ds(pl.multiple_of(p * 8, 8), 8)],
                dst,
                upd_send.at[q],
                upd_recv,
                at(row, col, p),
            )
            return carry

        lax.fori_loop(1, 16, go, 0)
        pltpu.make_async_copy(
            upd.at[q, pl.ds(pl.multiple_of(chan * 8, 8), 8)], dst, upd_recv
        ).start()

    finish(0)
    finish(1)

    wait(enc.at[0, :15], enc_send.at[0])
    wait(enc.at[1, :15], enc_send.at[1])
    wait(plane.at[0, :14], hid_send.at[0])
    wait(plane.at[1, :14], hid_send.at[1])
    for q in range(2):
        wait(upd.at[q, :120], upd_send.at[q])
    sent(L0)
    sent(L1)
    for s in range(4):

        @pl.when(core == s % 2)
        def _():
            wait(across.at[s, :15], plane_send.at[s])

        @pl.when(core != s % 2)
        def _():
            wait(across.at[s], plane_send.at[s])

    wait(rights.at[core], twin_send)
    wait(product.at[: 31 * 16], prod_send)
    wait(owned, upd_recv)
    out[...] = owned[...]


def shards(
    pair,
    pair_mask,
    norm_gain,
    norm_bias,
    in_weight,
    gate_weight,
    hidden_gain,
    hidden_bias,
    out_weight,
):
    bf16, f32 = jnp.bfloat16, jnp.float32
    dma = pltpu.SemaphoreType.DMA
    vmem = pl.BlockSpec(memory_space=pltpu.VMEM)
    update = pl.pallas_call(
        kernel,
        out_shape=jax.ShapeDtypeStruct((8, 128, 512), bf16),
        in_specs=[pl.BlockSpec(memory_space=pltpu.HBM)] * 9,
        out_specs=vmem,
        scratch_shapes=[
            pltpu.VMEM((2, 4, 8, 16, 512), f32),
            pltpu.VMEM((32, 128), jnp.int32),
            pltpu.VMEM((1, 128), f32),
            pltpu.VMEM((1, 128), f32),
            pltpu.VMEM((128, 512), bf16),
            pltpu.VMEM((128, 128), bf16),
            pltpu.VMEM((1, 128), f32),
            pltpu.VMEM((1, 128), f32),
            pltpu.VMEM((128, 128), bf16),
            pltpu.VMEM((2, 16, 8, 16, 128), jnp.int16),
            pltpu.VMEM((2, 128, 16, 128), jnp.int16),
            pltpu.VMEM((2048, 128), f32),
            pltpu.VMEM((2048, 128), f32),
            pltpu.VMEM((32, 128), f32),
            pltpu.VMEM((4, 128, 128), f32),
            pltpu.VMEM((640, 128), bf16),
            pltpu.VMEM((128, 256), bf16),
            pltpu.VMEM((4, 128, 16, 128), bf16),
            pltpu.VMEM((4, 16, 16, 1024), bf16),
            pltpu.VMEM((2, 512, 1024), bf16),
            pltpu.VMEM((512, 1024), bf16),
            pltpu.VMEM((512, 1024), bf16),
            pltpu.VMEM((2, 16, 16, 1024), bf16),
            pltpu.VMEM((2, 128, 16, 128), bf16),
            pltpu.VMEM((2, 16, 128, 128), f32),
            pltpu.VMEM((2, 128, 16, 128), bf16),
            pltpu.VMEM((8, 128, 512), bf16),
            dma((2,)),
            dma((8,)),
            dma((2,)),
            dma((2,)),
            dma((4,)),
            dma((4,)),
            dma((4,)),
            dma,
            dma,
            dma,
            dma,
            dma,
            dma((2,)),
            dma((2,)),
            dma((2,)),
            dma((2,)),
            dma,
        ],
        compiler_params=pltpu.CompilerParams(
            collective_id=0, has_side_effects=True, vmem_limit_bytes=62 * 2**20
        ),
        name="triangle",
    )(
        pair,
        pair_mask,
        norm_gain.reshape(1, 128),
        norm_bias.reshape(1, 128),
        in_weight,
        gate_weight,
        hidden_gain.reshape(1, 128),
        hidden_bias.reshape(1, 128),
        out_weight,
    )
    return update.astype(f32)


def solution(mesh):
    placed = (P("chan", "row", "col"), P("row", "col"), P(), P(), P(), P(), P(), P(), P())
    return jax.shard_map(
        shards, mesh=mesh, in_specs=placed, out_specs=P("chan", "row", "col"), check_vma=False
    )
```

```python
import jax
import jax.numpy as jnp
from jax import lax
from jax.experimental import pallas as pl
from jax.experimental.pallas import tpu as pltpu
from jax.sharding import PartitionSpec as P

EPS = 1e-05
MESH = pl.DeviceIdType.MESH
STEP = 6.0 / 32767.0
R0, R1, L0, L1 = range(4)


def kernel(
    pair_in,
    mask_in,
    norm_gain_in,
    norm_bias_in,
    in_weight_in,
    gate_weight_in,
    hidden_gain_in,
    hidden_bias_in,
    out_weight_in,
    out,
    pair,
    mask,
    norm_gain,
    norm_bias,
    in_weight,
    gate_weight,
    hidden_gain,
    hidden_bias,
    out_weight,
    enc,
    got,
    flat,
    flat2,
    maskf,
    columns,
    wt,
    pieces,
    sides,
    across,
    rights,
    lefts,
    product,
    plane,
    hidden,
    gate,
    upd,
    owned,
    pair_sem,
    load_sem,
    enc_send,
    enc_recv,
    side_send,
    side_recv,
    plane_send,
    right_recv,
    left_recv,
    twin_send,
    twin_recv,
    prod_send,
    prod_recv,
    hid_send,
    hid_recv,
    upd_send,
    upd_recv,
):
    row, col, chan = lax.axis_index("row"), lax.axis_index("col"), lax.axis_index("chan")
    x, core = row // 2, lax.rem(row, 2)
    y, zhi = chan // 4, lax.rem(chan, 4)
    z = zhi * 2 + col

    def at(r, c, h):
        return {"row": r, "col": c, "chan": h}

    def wait(ref, sem):
        pltpu.make_async_copy(ref, ref, sem).wait()

    def remote(src, dst, send, recv, device):
        pltpu.make_async_remote_copy(
            src_ref=src,
            dst_ref=dst,
            send_sem=send,
            recv_sem=recv,
            device_id=device,
            device_id_type=MESH,
        ).start()

    def block_of(zz):
        return pl.ds(pl.multiple_of((lax.rem(zz, 2) * 4 + zz // 2) * 128, 128), 128)

    for q in range(2):
        for k in range(4):
            pltpu.make_async_copy(
                pair_in.at[:, k * 32 + q * 16 : k * 32 + q * 16 + 16], pair.at[q, k], pair_sem.at[q]
            ).start()
    rows_mine = pl.ds(pl.multiple_of(y * 32, 32), 32)
    loads = [
        pltpu.make_async_copy(src, dst, load_sem.at[n])
        for n, (src, dst) in enumerate(
            [
                (mask_in.at[rows_mine, pl.ds(pl.multiple_of(zhi * 128, 128), 128)], mask),
                (norm_gain_in, norm_gain),
                (norm_bias_in, norm_bias),
                (in_weight_in, in_weight),
                (gate_weight_in, gate_weight),
                (hidden_gain_in, hidden_gain),
                (hidden_bias_in, hidden_bias),
                (out_weight_in, out_weight),
            ]
        )
    ]
    for load in loads:
        load.start()

    barrier = pltpu.get_barrier_semaphore()

    def greet(device):
        pl.semaphore_signal(barrier, inc=1, device_id=device, device_id_type=MESH)

    def greet_chan(t, carry):
        greet(at(row, col, lax.rem(chan + t, 16)))
        return carry

    def greet_z(t, carry):
        greet(at(row, 1 - col, y * 4 + t))
        return carry

    def greet_plane(t, carry):
        greet(at(lax.rem(row + 1 + t // 4, 8), col, lax.rem(t, 4) * 4 + zhi))
        return carry

    lax.fori_loop(1, 16, greet_chan, 0)
    lax.fori_loop(0, 4, greet_z, 0)
    lax.fori_loop(0, 28, greet_plane, 0)

    def encode(q):
        wait(pair.at[q], pair_sem.at[q])
        for p in range(16):
            part = pair[q, p // 4, :, :, (p % 4) * 128 : (p % 4) * 128 + 128]
            enc[q, p] = jnp.round(part * (1.0 / STEP)).astype(jnp.int32).astype(jnp.int16)

    def send_enc(q):
        mine = pl.ds(pl.multiple_of(chan * 8, 8), 8)

        def go(t, carry):
            p = lax.rem(chan + t, 16)
            if q == 1:
                wait(enc.at[0, 0], enc_send.at[t])
            remote(
                enc.at[q, p],
                got.at[q, mine],
                enc_send.at[t if q == 0 else 0],
                enc_recv.at[q],
                at(row, col, p),
            )
            return carry

        lax.fori_loop(1, 16, go, 0)
        pltpu.make_async_copy(enc.at[q, chan], got.at[q, mine], enc_recv.at[q]).start()

    encode(0)
    pl.semaphore_wait(barrier, 47)
    send_enc(0)
    encode(1)
    send_enc(1)

    for load in loads:
        load.wait()
    wt[:512] = in_weight[...].astype(jnp.float32).T.astype(jnp.bfloat16)
    wt[512:] = gate_weight[...].astype(jnp.float32).T.astype(jnp.bfloat16)
    columns[0] = jnp.broadcast_to(norm_gain[...], (128, 128)).T
    columns[1] = jnp.broadcast_to(norm_bias[...], (128, 128)).T
    out_t = out_weight[...].astype(jnp.float32).T
    scaled = out_t * hidden_gain[...]
    high = scaled.astype(jnp.bfloat16)
    low = (scaled - high.astype(jnp.float32)).astype(jnp.bfloat16)
    pieces[:, :128] = high
    pieces[:, 128:] = low
    total = jnp.sum(high.astype(jnp.float32) + low.astype(jnp.float32), axis=1, keepdims=True)
    columns[2] = jnp.broadcast_to(total, (128, 128))
    offset = jnp.sum(out_t * hidden_bias[...], axis=1, keepdims=True)
    columns[3] = jnp.broadcast_to(offset, (128, 128))
    maskf[...] = mask[...].astype(jnp.float32)

    def twice(a):
        return jnp.concatenate([a, a], axis=1)

    def rows_of(ref, i):
        return jnp.concatenate(
            [ref[pl.ds(2 * i, 128, stride=16), :], ref[pl.ds(2 * i + 1, 128, stride=16), :]],
            axis=1,
        )

    def put_rows(ref, i, value):
        ref[pl.ds(2 * i, 128, stride=16), :] = value[:, :128]
        ref[pl.ds(2 * i + 1, 128, stride=16), :] = value[:, 128:]

    def project(q):
        flat[...] = got[q].astype(jnp.int32).astype(jnp.float32).reshape(2048, 128) * STEP

        def step(i, carry):
            value = rows_of(flat, i)
            mean = jnp.sum(value, axis=0, keepdims=True) * (1.0 / 128)
            centred = value - mean
            var = jnp.sum(centred * centred, axis=0, keepdims=True) * (1.0 / 128)
            normed = centred * lax.rsqrt(var + EPS) * twice(columns[0]) + twice(columns[1])
            normed = normed.astype(jnp.bfloat16)
            present = jnp.concatenate(
                [
                    maskf[pl.ds(q * 16 + 2 * i, 1), :],
                    maskf[pl.ds(q * 16 + 2 * i + 1, 1), :],
                ],
                axis=1,
            )

            def proj(k):
                return jnp.dot(
                    wt[k * 128 : k * 128 + 128, :], normed, preferred_element_type=jnp.float32
                )

            put_rows(flat, i, jax.nn.sigmoid(proj(0)) * proj(1) * present)
            put_rows(flat2, i, jax.nn.sigmoid(proj(2)) * proj(3) * present)
            gated = jax.nn.sigmoid(proj(4))
            gate[q, 2 * i] = gated[:, :128]
            gate[q, 2 * i + 1] = gated[:, 128:]
            return carry

        lax.fori_loop(0, 8, step, 0)
        sides[L0 + q] = flat[...].reshape(128, 16, 128).astype(jnp.bfloat16)
        sides[R0 + q] = flat2[...].reshape(128, 16, 128).astype(jnp.bfloat16)

    def send_sides(s):
        def go(t, carry):
            zz = lax.rem(z + lax.select(lax.rem(t, 2) == 1, (9 - t) // 2, 4 + t // 2), 8)
            remote(
                sides.at[s, pl.ds(pl.multiple_of(zz * 16, 16), 16)],
                across.at[s, :, :, block_of(z)],
                side_send.at[s],
                side_recv.at[s],
                at(row, lax.rem(zz, 2), y * 4 + zz // 2),
            )
            return carry

        lax.fori_loop(1, 8, go, 0)
        pltpu.make_async_copy(
            sides.at[s, pl.ds(pl.multiple_of(z * 16, 16), 16)],
            across.at[s, :, :, block_of(z)],
            side_recv.at[s],
        ).start()

    def send_plane(s):
        q = s % 2
        ours = pl.ds(pl.multiple_of((row * 4 + y) * 16, 16), 16)
        dst = rights.at[q, ours] if s < L0 else lefts.at[ours]
        recv = right_recv if s < L0 else left_recv
        wait(across.at[s], side_recv.at[s])

        def go(t, carry):
            k = lax.rem(x * 4 + y + t, 16)
            remote(
                across.at[s, k],
                dst,
                plane_send.at[s],
                recv,
                at((k // 4) * 2 + q, col, lax.rem(k, 4) * 4 + zhi),
            )
            return carry

        lax.fori_loop(1, 16, go, 0)

        @pl.when(core == q)
        def _():
            pltpu.make_async_copy(across.at[s, x * 4 + y], dst, recv).start()

        @pl.when(core != q)
        def _():
            go(0, 0)

    def sent(s):
        wait(sides.at[s, :112], side_send.at[s])

    wait(got.at[0], enc_recv.at[0])
    project(0)
    send_sides(R0)
    wait(got.at[1], enc_recv.at[1])
    project(1)
    send_sides(R1)
    sent(R0)
    send_sides(L0)
    send_plane(R0)
    sent(R1)
    send_sides(L1)
    send_plane(R1)

    wait(rights.at[core], right_recv)
    remote(rights.at[core], rights.at[core], twin_send, twin_recv, at(x * 2 + 1 - core, col, chan))
    send_plane(L0)

    def multiply():
        wait(rights.at[1 - core], twin_recv)
        wait(lefts, left_recv)

        def step(m, carry):
            n = lax.rem(m + z // 2, 4)
            parts = []
            for half in range(2):
                for yy in range(4):
                    for q in range(2):
                        start = pl.multiple_of((n * 2 + half) * 64 + yy * 16, 16)
                        parts.append(rights[q, pl.ds(start, 16), :])
            block = jnp.concatenate(parts, axis=0)
            result = lax.dot_general(
                lefts[...], block, (((1,), (1,)), ((), ())), preferred_element_type=jnp.float32
            )
            span = pl.ds(pl.multiple_of(n * 256, 256), 256)
            product[:, span] = result.astype(jnp.bfloat16)

            def go(t, carry):
                k = lax.rem(row * 4 + y + t, 32)
                remote(
                    product.at[pl.ds(pl.multiple_of(k * 16, 16), 16), span],
                    plane.at[core, x * 4 + y, :, span],
                    prod_send.at[n],
                    prod_recv.at[core, n],
                    at(k // 4, col, lax.rem(k, 4) * 4 + zhi),
                )
                return carry

            lax.fori_loop(1, 32, go, 0)
            pltpu.make_async_copy(
                product.at[pl.ds(pl.multiple_of((row * 4 + y) * 16, 16), 16), span],
                plane.at[core, x * 4 + y, :, span],
                prod_recv.at[core, n],
            ).start()
            return carry

        lax.fori_loop(0, 4, step, 0)

    def send_hidden(q):
        dst = hidden.at[q, pl.ds(pl.multiple_of(z * 16, 16), 16)]

        def go(m, carry):
            n = lax.rem(m + z // 2, 4)
            span = pl.ds(pl.multiple_of(n * 256, 256), 256)
            wait(plane.at[q, :, :, span], prod_recv.at[q, n])
            for half in range(2):
                block = n * 2 + half
                zz = lax.rem(block, 4) * 2 + block // 4
                src = plane.at[q, :, :, pl.ds(pl.multiple_of(block * 128, 128), 128)]

                @pl.when(zz == z)
                def _():
                    pltpu.make_async_copy(src, dst, hid_recv.at[q]).start()

                @pl.when(zz != z)
                def _():
                    remote(
                        src,
                        dst,
                        hid_send.at[q],
                        hid_recv.at[q],
                        at(row, lax.rem(zz, 2), y * 4 + zz // 2),
                    )

            return carry

        lax.fori_loop(0, 4, go, 0)

    @pl.when(core == 0)
    def _():
        multiply()

    send_plane(L1)
    send_hidden(0)

    @pl.when(core == 1)
    def _():
        multiply()

    send_hidden(1)

    def finish(q):
        wait(hidden.at[q], hid_recv.at[q])
        flat[...] = hidden[q].astype(jnp.float32).reshape(2048, 128)

        def step(i, carry):
            value = rows_of(flat, i)
            nu = jnp.sum(value, axis=0, keepdims=True) * (1.0 / 128)
            dev = value - nu
            tau = jnp.sum(dev * dev, axis=0, keepdims=True) * (1.0 / 128)
            short = value.astype(jnp.bfloat16)
            raw = jnp.dot(
                pieces[...],
                jnp.concatenate([short, short], axis=0),
                preferred_element_type=jnp.float32,
            )
            out_rows = (raw - twice(columns[2]) * nu) * lax.rsqrt(tau + EPS) + twice(columns[3])
            gated = jnp.concatenate([gate[q, 2 * i], gate[q, 2 * i + 1]], axis=1)
            put_rows(flat2, i, gated * out_rows)
            return carry

        lax.fori_loop(0, 8, step, 0)
        upd[q] = flat2[...].reshape(128, 16, 128).astype(jnp.bfloat16)
        dst = owned.at[
            :,
            pl.ds(pl.multiple_of(y * 32 + q * 16, 16), 16),
            pl.ds(pl.multiple_of(zhi * 128, 128), 128),
        ]

        def go(t, carry):
            p = lax.rem(chan + t, 16)
            remote(
                upd.at[q, pl.ds(pl.multiple_of(p * 8, 8), 8)],
                dst,
                upd_send.at[q],
                upd_recv,
                at(row, col, p),
            )
            return carry

        lax.fori_loop(1, 16, go, 0)
        pltpu.make_async_copy(
            upd.at[q, pl.ds(pl.multiple_of(chan * 8, 8), 8)], dst, upd_recv
        ).start()

    finish(0)
    finish(1)

    wait(enc.at[1, :15], enc_send.at[0])
    wait(plane.at[0, :14], hid_send.at[0])
    wait(plane.at[1, :14], hid_send.at[1])
    for q in range(2):
        wait(upd.at[q, :120], upd_send.at[q])
    sent(L0)
    sent(L1)
    for s in range(4):

        @pl.when(core == s % 2)
        def _():
            wait(across.at[s, :15], plane_send.at[s])

        @pl.when(core != s % 2)
        def _():
            wait(across.at[s], plane_send.at[s])

    wait(rights.at[core], twin_send)
    for n in range(4):
        wait(product.at[:496, :256], prod_send.at[n])
    wait(owned, upd_recv)
    out[...] = owned[...]


def shards(
    pair,
    pair_mask,
    norm_gain,
    norm_bias,
    in_weight,
    gate_weight,
    hidden_gain,
    hidden_bias,
    out_weight,
):
    bf16, f32 = jnp.bfloat16, jnp.float32
    dma = pltpu.SemaphoreType.DMA
    vmem = pl.BlockSpec(memory_space=pltpu.VMEM)
    update = pl.pallas_call(
        kernel,
        out_shape=jax.ShapeDtypeStruct((8, 128, 512), bf16),
        in_specs=[pl.BlockSpec(memory_space=pltpu.HBM)] * 9,
        out_specs=vmem,
        scratch_shapes=[
            pltpu.VMEM((2, 4, 8, 16, 512), f32),
            pltpu.VMEM((32, 128), jnp.int32),
            pltpu.VMEM((1, 128), f32),
            pltpu.VMEM((1, 128), f32),
            pltpu.VMEM((128, 512), bf16),
            pltpu.VMEM((128, 128), bf16),
            pltpu.VMEM((1, 128), f32),
            pltpu.VMEM((1, 128), f32),
            pltpu.VMEM((128, 128), bf16),
            pltpu.VMEM((2, 16, 8, 16, 128), jnp.int16),
            pltpu.VMEM((2, 128, 16, 128), jnp.int16),
            pltpu.VMEM((2048, 128), f32),
            pltpu.VMEM((2048, 128), f32),
            pltpu.VMEM((32, 128), f32),
            pltpu.VMEM((4, 128, 128), f32),
            pltpu.VMEM((640, 128), bf16),
            pltpu.VMEM((128, 256), bf16),
            pltpu.VMEM((4, 128, 16, 128), bf16),
            pltpu.VMEM((4, 16, 16, 1024), bf16),
            pltpu.VMEM((2, 512, 1024), bf16),
            pltpu.VMEM((512, 1024), bf16),
            pltpu.VMEM((512, 1024), bf16),
            pltpu.VMEM((2, 16, 16, 1024), bf16),
            pltpu.VMEM((2, 128, 16, 128), bf16),
            pltpu.VMEM((2, 16, 128, 128), f32),
            pltpu.VMEM((2, 128, 16, 128), bf16),
            pltpu.VMEM((8, 128, 512), bf16),
            dma((2,)),
            dma((8,)),
            dma((16,)),
            dma((2,)),
            dma((4,)),
            dma((4,)),
            dma((4,)),
            dma,
            dma,
            dma,
            dma,
            dma((4,)),
            dma((2, 4)),
            dma((2,)),
            dma((2,)),
            dma((2,)),
            dma,
        ],
        compiler_params=pltpu.CompilerParams(
            collective_id=0, has_side_effects=True, vmem_limit_bytes=62 * 2**20
        ),
        name="triangle",
    )(
        pair,
        pair_mask,
        norm_gain.reshape(1, 128),
        norm_bias.reshape(1, 128),
        in_weight,
        gate_weight,
        hidden_gain.reshape(1, 128),
        hidden_bias.reshape(1, 128),
        out_weight,
    )
    return update.astype(f32)


def solution(mesh):
    placed = (P("chan", "row", "col"), P("row", "col"), P(), P(), P(), P(), P(), P(), P())
    return jax.shard_map(
        shards, mesh=mesh, in_specs=placed, out_specs=P("chan", "row", "col"), check_vma=False
    )
```

```python
import jax
import jax.numpy as jnp
from jax import lax
from jax.experimental import pallas as pl
from jax.experimental.pallas import tpu as pltpu
from jax.sharding import PartitionSpec as P

EPS = 1e-05
MESH = pl.DeviceIdType.MESH
STEP = 6.0 / 32767.0
R0, R1, L0, L1 = range(4)


def kernel(
    pair_in,
    mask_in,
    norm_gain_in,
    norm_bias_in,
    in_weight_in,
    gate_weight_in,
    hidden_gain_in,
    hidden_bias_in,
    out_weight_in,
    out,
    pair,
    mask,
    norm_gain,
    norm_bias,
    in_weight,
    gate_weight,
    hidden_gain,
    hidden_bias,
    out_weight,
    enc,
    got,
    flat,
    flat2,
    maskf,
    columns,
    wt,
    pieces,
    sides,
    across,
    rights,
    lefts,
    product,
    plane,
    hidden,
    gate,
    upd,
    owned,
    pair_sem,
    load_sem,
    enc_send,
    enc_recv,
    side_send,
    side_recv,
    plane_send,
    right_recv,
    left_recv,
    twin_send,
    twin_recv,
    prod_send,
    prod_recv,
    hid_send,
    hid_recv,
    upd_send,
    upd_recv,
):
    row, col, chan = lax.axis_index("row"), lax.axis_index("col"), lax.axis_index("chan")
    x, core = row // 2, lax.rem(row, 2)
    y, zhi = chan // 4, lax.rem(chan, 4)
    z = zhi * 2 + col

    def at(r, c, h):
        return {"row": r, "col": c, "chan": h}

    def wait(ref, sem):
        pltpu.make_async_copy(ref, ref, sem).wait()

    def remote(src, dst, send, recv, device):
        pltpu.make_async_remote_copy(
            src_ref=src,
            dst_ref=dst,
            send_sem=send,
            recv_sem=recv,
            device_id=device,
            device_id_type=MESH,
        ).start()

    def block_of(zz):
        return pl.ds(pl.multiple_of((lax.rem(zz, 2) * 4 + zz // 2) * 128, 128), 128)

    for q in range(2):
        for k in range(4):
            pltpu.make_async_copy(
                pair_in.at[:, k * 32 + q * 16 : k * 32 + q * 16 + 16], pair.at[q, k], pair_sem.at[q]
            ).start()
    rows_mine = pl.ds(pl.multiple_of(y * 32, 32), 32)
    loads = [
        pltpu.make_async_copy(src, dst, load_sem.at[n])
        for n, (src, dst) in enumerate(
            [
                (mask_in.at[rows_mine, pl.ds(pl.multiple_of(zhi * 128, 128), 128)], mask),
                (norm_gain_in, norm_gain),
                (norm_bias_in, norm_bias),
                (in_weight_in, in_weight),
                (gate_weight_in, gate_weight),
                (hidden_gain_in, hidden_gain),
                (hidden_bias_in, hidden_bias),
                (out_weight_in, out_weight),
            ]
        )
    ]
    for load in loads:
        load.start()

    barrier = pltpu.get_barrier_semaphore()

    def greet(device):
        pl.semaphore_signal(barrier, inc=1, device_id=device, device_id_type=MESH)

    def greet_chan(t, carry):
        greet(at(row, col, lax.rem(chan + t, 16)))
        return carry

    def greet_z(t, carry):
        greet(at(row, 1 - col, y * 4 + t))
        return carry

    def greet_plane(t, carry):
        greet(at(lax.rem(row + 1 + t // 4, 8), col, lax.rem(t, 4) * 4 + zhi))
        return carry

    lax.fori_loop(1, 16, greet_chan, 0)
    lax.fori_loop(0, 4, greet_z, 0)
    lax.fori_loop(0, 28, greet_plane, 0)

    def encode(q):
        wait(pair.at[q], pair_sem.at[q])
        for p in range(16):
            part = pair[q, p // 4, :, :, (p % 4) * 128 : (p % 4) * 128 + 128]
            enc[q, p] = jnp.round(part * (1.0 / STEP)).astype(jnp.int32).astype(jnp.int16)

    def send_enc(q):
        mine = pl.ds(pl.multiple_of(chan * 8, 8), 8)

        def go(t, carry):
            p = lax.rem(chan + t, 16)
            if q == 1:
                wait(enc.at[0, 0], enc_send.at[t])
            remote(
                enc.at[q, p],
                got.at[q, mine],
                enc_send.at[t if q == 0 else 0],
                enc_recv.at[q],
                at(row, col, p),
            )
            return carry

        lax.fori_loop(1, 16, go, 0)
        pltpu.make_async_copy(enc.at[q, chan], got.at[q, mine], enc_recv.at[q]).start()

    encode(0)
    pl.semaphore_wait(barrier, 47)
    send_enc(0)
    encode(1)
    send_enc(1)

    for load in loads:
        load.wait()
    wt[:512] = in_weight[...].astype(jnp.float32).T.astype(jnp.bfloat16)
    wt[512:] = gate_weight[...].astype(jnp.float32).T.astype(jnp.bfloat16)
    columns[0] = jnp.broadcast_to(norm_gain[...], (128, 128)).T
    columns[1] = jnp.broadcast_to(norm_bias[...], (128, 128)).T
    out_t = out_weight[...].astype(jnp.float32).T
    scaled = out_t * hidden_gain[...]
    high = scaled.astype(jnp.bfloat16)
    low = (scaled - high.astype(jnp.float32)).astype(jnp.bfloat16)
    pieces[:, :128] = high
    pieces[:, 128:] = low
    total = jnp.sum(high.astype(jnp.float32) + low.astype(jnp.float32), axis=1, keepdims=True)
    columns[2] = jnp.broadcast_to(total, (128, 128))
    offset = jnp.sum(out_t * hidden_bias[...], axis=1, keepdims=True)
    columns[3] = jnp.broadcast_to(offset, (128, 128))
    maskf[...] = mask[...].astype(jnp.float32)

    def twice(a):
        return jnp.concatenate([a, a], axis=1)

    def rows_of(ref, i):
        return jnp.concatenate(
            [ref[pl.ds(2 * i, 128, stride=16), :], ref[pl.ds(2 * i + 1, 128, stride=16), :]],
            axis=1,
        )

    def put_rows(ref, i, value):
        ref[pl.ds(2 * i, 128, stride=16), :] = value[:, :128]
        ref[pl.ds(2 * i + 1, 128, stride=16), :] = value[:, 128:]

    def project(q):
        flat[...] = got[q].astype(jnp.int32).astype(jnp.float32).reshape(2048, 128) * STEP

        def step(i, carry):
            value = rows_of(flat, i)
            mean = jnp.sum(value, axis=0, keepdims=True) * (1.0 / 128)
            centred = value - mean
            var = jnp.sum(centred * centred, axis=0, keepdims=True) * (1.0 / 128)
            normed = centred * lax.rsqrt(var + EPS) * twice(columns[0]) + twice(columns[1])
            normed = normed.astype(jnp.bfloat16)
            present = jnp.concatenate(
                [
                    maskf[pl.ds(q * 16 + 2 * i, 1), :],
                    maskf[pl.ds(q * 16 + 2 * i + 1, 1), :],
                ],
                axis=1,
            )

            def proj(k):
                return jnp.dot(
                    wt[k * 128 : k * 128 + 128, :], normed, preferred_element_type=jnp.float32
                )

            put_rows(flat, i, jax.nn.sigmoid(proj(0)) * proj(1) * present)
            put_rows(flat2, i, jax.nn.sigmoid(proj(2)) * proj(3) * present)
            gated = jax.nn.sigmoid(proj(4))
            gate[q, 2 * i] = gated[:, :128]
            gate[q, 2 * i + 1] = gated[:, 128:]
            return carry

        lax.fori_loop(0, 8, step, 0)
        sides[L0 + q] = flat[...].reshape(128, 16, 128).astype(jnp.bfloat16)
        sides[R0 + q] = flat2[...].reshape(128, 16, 128).astype(jnp.bfloat16)

    def send_sides(s, g):
        mine = pl.ds(g * 8, 8)

        def go(t, carry):
            zz = lax.rem(z + lax.select(lax.rem(t, 2) == 1, (9 - t) // 2, 4 + t // 2), 8)
            remote(
                sides.at[s, pl.ds(pl.multiple_of(zz * 16 + g * 8, 8), 8)],
                across.at[s, mine, :, block_of(z)],
                side_send.at[s, g],
                side_recv.at[s, g],
                at(row, lax.rem(zz, 2), y * 4 + zz // 2),
            )
            return carry

        lax.fori_loop(1, 8, go, 0)
        pltpu.make_async_copy(
            sides.at[s, pl.ds(pl.multiple_of(z * 16 + g * 8, 8), 8)],
            across.at[s, mine, :, block_of(z)],
            side_recv.at[s, g],
        ).start()

    def sent(s, g):
        wait(sides.at[s, :56], side_send.at[s, g])

    def send_plane(s, g):
        q = s % 2
        ours = pl.ds(pl.multiple_of((row * 4 + y) * 16, 16), 16)
        dst = rights.at[q, ours] if s < L0 else lefts.at[ours]
        recv = right_recv if s < L0 else left_recv
        wait(across.at[s, g * 8 : g * 8 + 8], side_recv.at[s, g])

        def go(t, carry):
            k = lax.rem(x * 2 + y // 2 + t, 8)
            remote(
                across.at[s, g * 8 + k],
                dst,
                plane_send.at[s],
                recv,
                at((k // 2) * 2 + q, col, (lax.rem(k, 2) * 2 + g) * 4 + zhi),
            )
            return carry

        lax.fori_loop(1, 8, go, 0)
        here = jnp.logical_and(core == q, lax.rem(y, 2) == g)

        @pl.when(here)
        def _():
            pltpu.make_async_copy(across.at[s, g * 8 + x * 2 + y // 2], dst, recv).start()

        @pl.when(jnp.logical_not(here))
        def _():
            go(0, 0)

    wait(got.at[0], enc_recv.at[0])
    project(0)
    send_sides(R0, 0)
    send_sides(R0, 1)
    wait(got.at[1], enc_recv.at[1])
    project(1)
    send_sides(R1, 0)
    send_sides(R1, 1)
    for g in range(2):
        sent(R0, g)
        send_sides(L0, g)
        send_plane(R0, g)
    sent(R1, 0)
    sent(R1, 1)
    send_plane(R1, 0)
    send_plane(R1, 1)
    for g in range(2):
        sent(L0, g)
        send_sides(L1, g)

    wait(rights.at[core], right_recv)
    remote(rights.at[core], rights.at[core], twin_send, twin_recv, at(x * 2 + 1 - core, col, chan))
    send_plane(L0, 0)
    send_plane(L0, 1)
    place = lax.rem(y, 2) * 8 + x * 2 + y // 2

    def multiply():
        wait(rights.at[1 - core], twin_recv)
        wait(lefts, left_recv)

        def step(m, carry):
            n = lax.rem(m + z // 2, 4)
            parts = []
            for half in range(2):
                for yy in range(4):
                    for q in range(2):
                        start = pl.multiple_of((n * 2 + half) * 64 + yy * 16, 16)
                        parts.append(rights[q, pl.ds(start, 16), :])
            block = jnp.concatenate(parts, axis=0)
            result = lax.dot_general(
                lefts[...], block, (((1,), (1,)), ((), ())), preferred_element_type=jnp.float32
            )
            span = pl.ds(pl.multiple_of(n * 256, 256), 256)
            product[:, span] = result.astype(jnp.bfloat16)

            def go(t, carry):
                k = lax.rem(row * 4 + y + t, 32)
                remote(
                    product.at[pl.ds(pl.multiple_of(k * 16, 16), 16), span],
                    plane.at[core, place, :, span],
                    prod_send.at[n],
                    prod_recv.at[core * 2 + lax.rem(y, 2), n],
                    at(k // 4, col, lax.rem(k, 4) * 4 + zhi),
                )
                return carry

            lax.fori_loop(1, 32, go, 0)
            pltpu.make_async_copy(
                product.at[pl.ds(pl.multiple_of((row * 4 + y) * 16, 16), 16), span],
                plane.at[core, place, :, span],
                prod_recv.at[core * 2 + lax.rem(y, 2), n],
            ).start()
            return carry

        lax.fori_loop(0, 4, step, 0)

    def send_hidden(q, g):
        part = pl.ds(g * 8, 8)
        dst = hidden.at[q, pl.ds(pl.multiple_of(z * 16 + g * 8, 8), 8)]

        def go(m, carry):
            n = lax.rem(m + z // 2, 4)
            span = pl.ds(pl.multiple_of(n * 256, 256), 256)
            wait(plane.at[q, part, :, span], prod_recv.at[q * 2 + g, n])
            for half in range(2):
                block = n * 2 + half
                zz = lax.rem(block, 4) * 2 + block // 4
                src = plane.at[q, part, :, pl.ds(pl.multiple_of(block * 128, 128), 128)]

                @pl.when(zz == z)
                def _():
                    pltpu.make_async_copy(src, dst, hid_recv.at[q]).start()

                @pl.when(zz != z)
                def _():
                    remote(
                        src,
                        dst,
                        hid_send.at[q],
                        hid_recv.at[q],
                        at(row, lax.rem(zz, 2), y * 4 + zz // 2),
                    )

            return carry

        lax.fori_loop(0, 4, go, 0)

    @pl.when(core == 0)
    def _():
        multiply()

    send_plane(L1, 0)
    send_hidden(0, 0)
    send_plane(L1, 1)
    send_hidden(0, 1)

    @pl.when(core == 1)
    def _():
        multiply()

    send_hidden(1, 0)
    send_hidden(1, 1)

    def finish(q):
        wait(hidden.at[q], hid_recv.at[q])
        flat[...] = hidden[q].astype(jnp.float32).reshape(2048, 128)

        def step(i, carry):
            value = rows_of(flat, i)
            nu = jnp.sum(value, axis=0, keepdims=True) * (1.0 / 128)
            dev = value - nu
            tau = jnp.sum(dev * dev, axis=0, keepdims=True) * (1.0 / 128)
            short = value.astype(jnp.bfloat16)
            raw = jnp.dot(
                pieces[...],
                jnp.concatenate([short, short], axis=0),
                preferred_element_type=jnp.float32,
            )
            out_rows = (raw - twice(columns[2]) * nu) * lax.rsqrt(tau + EPS) + twice(columns[3])
            gated = jnp.concatenate([gate[q, 2 * i], gate[q, 2 * i + 1]], axis=1)
            put_rows(flat2, i, gated * out_rows)
            return carry

        lax.fori_loop(0, 8, step, 0)
        upd[q] = flat2[...].reshape(128, 16, 128).astype(jnp.bfloat16)
        dst = owned.at[
            :,
            pl.ds(pl.multiple_of(y * 32 + q * 16, 16), 16),
            pl.ds(pl.multiple_of(zhi * 128, 128), 128),
        ]

        def go(t, carry):
            p = lax.rem(chan + t, 16)
            remote(
                upd.at[q, pl.ds(pl.multiple_of(p * 8, 8), 8)],
                dst,
                upd_send.at[q],
                upd_recv,
                at(row, col, p),
            )
            return carry

        lax.fori_loop(1, 16, go, 0)
        pltpu.make_async_copy(
            upd.at[q, pl.ds(pl.multiple_of(chan * 8, 8), 8)], dst, upd_recv
        ).start()

    finish(0)
    finish(1)

    wait(enc.at[1, :15], enc_send.at[0])
    wait(plane.at[0, :14], hid_send.at[0])
    wait(plane.at[1, :14], hid_send.at[1])
    for q in range(2):
        wait(upd.at[q, :120], upd_send.at[q])
    for g in range(2):
        sent(L1, g)
    for s in range(4):

        @pl.when(core == s % 2)
        def _():
            wait(across.at[s, :15], plane_send.at[s])

        @pl.when(core != s % 2)
        def _():
            wait(across.at[s], plane_send.at[s])

    wait(rights.at[core], twin_send)
    for n in range(4):
        wait(product.at[:496, :256], prod_send.at[n])
    wait(owned, upd_recv)
    out[...] = owned[...]


def shards(
    pair,
    pair_mask,
    norm_gain,
    norm_bias,
    in_weight,
    gate_weight,
    hidden_gain,
    hidden_bias,
    out_weight,
):
    bf16, f32 = jnp.bfloat16, jnp.float32
    dma = pltpu.SemaphoreType.DMA
    vmem = pl.BlockSpec(memory_space=pltpu.VMEM)
    update = pl.pallas_call(
        kernel,
        out_shape=jax.ShapeDtypeStruct((8, 128, 512), bf16),
        in_specs=[pl.BlockSpec(memory_space=pltpu.HBM)] * 9,
        out_specs=vmem,
        scratch_shapes=[
            pltpu.VMEM((2, 4, 8, 16, 512), f32),
            pltpu.VMEM((32, 128), jnp.int32),
            pltpu.VMEM((1, 128), f32),
            pltpu.VMEM((1, 128), f32),
            pltpu.VMEM((128, 512), bf16),
            pltpu.VMEM((128, 128), bf16),
            pltpu.VMEM((1, 128), f32),
            pltpu.VMEM((1, 128), f32),
            pltpu.VMEM((128, 128), bf16),
            pltpu.VMEM((2, 16, 8, 16, 128), jnp.int16),
            pltpu.VMEM((2, 128, 16, 128), jnp.int16),
            pltpu.VMEM((2048, 128), f32),
            pltpu.VMEM((2048, 128), f32),
            pltpu.VMEM((32, 128), f32),
            pltpu.VMEM((4, 128, 128), f32),
            pltpu.VMEM((640, 128), bf16),
            pltpu.VMEM((128, 256), bf16),
            pltpu.VMEM((4, 128, 16, 128), bf16),
            pltpu.VMEM((4, 16, 16, 1024), bf16),
            pltpu.VMEM((2, 512, 1024), bf16),
            pltpu.VMEM((512, 1024), bf16),
            pltpu.VMEM((512, 1024), bf16),
            pltpu.VMEM((2, 16, 16, 1024), bf16),
            pltpu.VMEM((2, 128, 16, 128), bf16),
            pltpu.VMEM((2, 16, 128, 128), f32),
            pltpu.VMEM((2, 128, 16, 128), bf16),
            pltpu.VMEM((8, 128, 512), bf16),
            dma((2,)),
            dma((8,)),
            dma((16,)),
            dma((2,)),
            dma((4, 2)),
            dma((4, 2)),
            dma((4,)),
            dma,
            dma,
            dma,
            dma,
            dma((4,)),
            dma((4, 4)),
            dma((2,)),
            dma((2,)),
            dma((2,)),
            dma,
        ],
        compiler_params=pltpu.CompilerParams(
            collective_id=0, has_side_effects=True, vmem_limit_bytes=62 * 2**20
        ),
        name="triangle",
    )(
        pair,
        pair_mask,
        norm_gain.reshape(1, 128),
        norm_bias.reshape(1, 128),
        in_weight,
        gate_weight,
        hidden_gain.reshape(1, 128),
        hidden_bias.reshape(1, 128),
        out_weight,
    )
    return update.astype(f32)


def solution(mesh):
    placed = (P("chan", "row", "col"), P("row", "col"), P(), P(), P(), P(), P(), P(), P())
    return jax.shard_map(
        shards, mesh=mesh, in_specs=placed, out_specs=P("chan", "row", "col"), check_vma=False
    )
```

```python
import jax
import jax.numpy as jnp
from jax import lax
from jax.experimental import pallas as pl
from jax.experimental.pallas import tpu as pltpu
from jax.sharding import PartitionSpec as P

EPS = 1e-05
MESH = pl.DeviceIdType.MESH
STEP = 6.0 / 32767.0
R0, R1, L0, L1 = range(4)


def kernel(
    pair_in,
    mask_in,
    norm_gain_in,
    norm_bias_in,
    in_weight_in,
    gate_weight_in,
    hidden_gain_in,
    hidden_bias_in,
    out_weight_in,
    out,
    pair,
    mask,
    norm_gain,
    norm_bias,
    in_weight,
    gate_weight,
    hidden_gain,
    hidden_bias,
    out_weight,
    enc,
    got,
    flat,
    flat2,
    maskf,
    columns,
    wt,
    pieces,
    sides,
    across,
    rights,
    lefts,
    product,
    plane,
    hidden,
    gate,
    upd,
    owned,
    pair_sem,
    load_sem,
    enc_send,
    enc_recv,
    side_send,
    side_recv,
    plane_send,
    right_recv,
    left_recv,
    twin_send,
    twin_recv,
    prod_send,
    prod_recv,
    hid_send,
    hid_recv,
    upd_send,
    upd_recv,
):
    row, col, chan = lax.axis_index("row"), lax.axis_index("col"), lax.axis_index("chan")
    x, core = row // 2, lax.rem(row, 2)
    y, zhi = chan // 4, lax.rem(chan, 4)
    z = zhi * 2 + col

    def at(r, c, h):
        return {"row": r, "col": c, "chan": h}

    def wait(ref, sem):
        pltpu.make_async_copy(ref, ref, sem).wait()

    def remote(src, dst, send, recv, device):
        pltpu.make_async_remote_copy(
            src_ref=src,
            dst_ref=dst,
            send_sem=send,
            recv_sem=recv,
            device_id=device,
            device_id_type=MESH,
        ).start()

    def block_of(zz):
        return pl.ds(pl.multiple_of((lax.rem(zz, 2) * 4 + zz // 2) * 128, 128), 128)

    for q in range(2):
        for k in range(4):
            pltpu.make_async_copy(
                pair_in.at[:, k * 32 + q * 16 : k * 32 + q * 16 + 16], pair.at[q, k], pair_sem.at[q]
            ).start()
    rows_mine = pl.ds(pl.multiple_of(y * 32, 32), 32)
    loads = [
        pltpu.make_async_copy(src, dst, load_sem.at[n])
        for n, (src, dst) in enumerate(
            [
                (mask_in.at[rows_mine, pl.ds(pl.multiple_of(zhi * 128, 128), 128)], mask),
                (norm_gain_in, norm_gain),
                (norm_bias_in, norm_bias),
                (in_weight_in, in_weight),
                (gate_weight_in, gate_weight),
                (hidden_gain_in, hidden_gain),
                (hidden_bias_in, hidden_bias),
                (out_weight_in, out_weight),
            ]
        )
    ]
    for load in loads:
        load.start()

    barrier = pltpu.get_barrier_semaphore()

    def greet(device):
        pl.semaphore_signal(barrier, inc=1, device_id=device, device_id_type=MESH)

    def greet_chan(t, carry):
        greet(at(row, col, lax.rem(chan + t, 16)))
        return carry

    def greet_z(t, carry):
        greet(at(row, 1 - col, y * 4 + t))
        return carry

    def greet_plane(t, carry):
        greet(at(lax.rem(row + 1 + t // 4, 8), col, lax.rem(t, 4) * 4 + zhi))
        return carry

    lax.fori_loop(1, 16, greet_chan, 0)
    lax.fori_loop(0, 4, greet_z, 0)
    lax.fori_loop(0, 28, greet_plane, 0)

    def encode(q):
        wait(pair.at[q], pair_sem.at[q])
        for p in range(16):
            part = pair[q, p // 4, :, :, (p % 4) * 128 : (p % 4) * 128 + 128]
            enc[q, p] = jnp.round(part * (1.0 / STEP)).astype(jnp.int32).astype(jnp.int16)

    def send_enc(q):
        mine = pl.ds(pl.multiple_of(chan * 8, 8), 8)

        def go(t, carry):
            p = lax.rem(chan + t, 16)
            if q == 1:
                wait(enc.at[0, 0], enc_send.at[t])
            remote(
                enc.at[q, p],
                got.at[q, mine],
                enc_send.at[t if q == 0 else 0],
                enc_recv.at[q],
                at(row, col, p),
            )
            return carry

        lax.fori_loop(1, 16, go, 0)
        pltpu.make_async_copy(enc.at[q, chan], got.at[q, mine], enc_recv.at[q]).start()

    encode(0)
    pl.semaphore_wait(barrier, 47)
    send_enc(0)
    encode(1)
    send_enc(1)

    for load in loads:
        load.wait()
    wt[:512] = in_weight[...].astype(jnp.float32).T.astype(jnp.bfloat16)
    wt[512:] = gate_weight[...].astype(jnp.float32).T.astype(jnp.bfloat16)
    columns[0] = jnp.broadcast_to(norm_gain[...], (128, 128)).T
    columns[1] = jnp.broadcast_to(norm_bias[...], (128, 128)).T
    out_t = out_weight[...].astype(jnp.float32).T
    scaled = out_t * hidden_gain[...]
    high = scaled.astype(jnp.bfloat16)
    low = (scaled - high.astype(jnp.float32)).astype(jnp.bfloat16)
    pieces[:, :128] = high
    pieces[:, 128:] = low
    total = jnp.sum(high.astype(jnp.float32) + low.astype(jnp.float32), axis=1, keepdims=True)
    columns[2] = jnp.broadcast_to(total, (128, 128))
    offset = jnp.sum(out_t * hidden_bias[...], axis=1, keepdims=True)
    columns[3] = jnp.broadcast_to(offset, (128, 128))
    maskf[...] = mask[...].astype(jnp.float32)

    def twice(a):
        return jnp.concatenate([a, a], axis=1)

    def rows_of(ref, i):
        return jnp.concatenate(
            [ref[pl.ds(2 * i, 128, stride=16), :], ref[pl.ds(2 * i + 1, 128, stride=16), :]],
            axis=1,
        )

    def put_rows(ref, i, value):
        ref[pl.ds(2 * i, 128, stride=16), :] = value[:, :128]
        ref[pl.ds(2 * i + 1, 128, stride=16), :] = value[:, 128:]

    def project(q):
        flat[...] = got[q].astype(jnp.int32).astype(jnp.float32).reshape(2048, 128) * STEP

        def step(i, carry):
            value = rows_of(flat, i)
            mean = jnp.sum(value, axis=0, keepdims=True) * (1.0 / 128)
            centred = value - mean
            var = jnp.sum(centred * centred, axis=0, keepdims=True) * (1.0 / 128)
            normed = centred * lax.rsqrt(var + EPS) * twice(columns[0]) + twice(columns[1])
            normed = normed.astype(jnp.bfloat16)
            present = jnp.concatenate(
                [
                    maskf[pl.ds(q * 16 + 2 * i, 1), :],
                    maskf[pl.ds(q * 16 + 2 * i + 1, 1), :],
                ],
                axis=1,
            )

            def proj(k):
                return jnp.dot(
                    wt[k * 128 : k * 128 + 128, :], normed, preferred_element_type=jnp.float32
                )

            put_rows(flat, i, jax.nn.sigmoid(proj(0)) * proj(1) * present)
            put_rows(flat2, i, jax.nn.sigmoid(proj(2)) * proj(3) * present)
            gated = jax.nn.sigmoid(proj(4))
            gate[q, 2 * i] = gated[:, :128]
            gate[q, 2 * i + 1] = gated[:, 128:]
            return carry

        lax.fori_loop(0, 8, step, 0)
        sides[L0 + q] = flat[...].reshape(128, 16, 128).astype(jnp.bfloat16)
        sides[R0 + q] = flat2[...].reshape(128, 16, 128).astype(jnp.bfloat16)

    def send_sides(s, g):
        mine = pl.ds(g * 8, 8)

        def go(t, carry):
            zz = lax.rem(z + lax.select(lax.rem(t, 2) == 1, (9 - t) // 2, 4 + t // 2), 8)
            remote(
                sides.at[s, pl.ds(pl.multiple_of(zz * 16 + g * 8, 8), 8)],
                across.at[s, mine, :, block_of(z)],
                side_send.at[s, g],
                side_recv.at[s, g],
                at(row, lax.rem(zz, 2), y * 4 + zz // 2),
            )
            return carry

        lax.fori_loop(1, 8, go, 0)
        pltpu.make_async_copy(
            sides.at[s, pl.ds(pl.multiple_of(z * 16 + g * 8, 8), 8)],
            across.at[s, mine, :, block_of(z)],
            side_recv.at[s, g],
        ).start()

    def sent(s, g):
        wait(sides.at[s, :56], side_send.at[s, g])

    def send_plane(s, g):
        q = s % 2
        ours = pl.ds(pl.multiple_of((row * 4 + y) * 16, 16), 16)
        dst = rights.at[q, ours] if s < L0 else lefts.at[ours]
        recv = right_recv if s < L0 else left_recv
        wait(across.at[s, g * 8 : g * 8 + 8], side_recv.at[s, g])

        def go(t, carry):
            k = lax.rem(x * 2 + y // 2 + t, 8)
            remote(
                across.at[s, g * 8 + k],
                dst,
                plane_send.at[s],
                recv,
                at((k // 2) * 2 + q, col, (lax.rem(k, 2) * 2 + g) * 4 + zhi),
            )
            return carry

        lax.fori_loop(1, 8, go, 0)
        here = jnp.logical_and(core == q, lax.rem(y, 2) == g)

        @pl.when(here)
        def _():
            pltpu.make_async_copy(across.at[s, g * 8 + x * 2 + y // 2], dst, recv).start()

        @pl.when(jnp.logical_not(here))
        def _():
            go(0, 0)

    wait(got.at[0], enc_recv.at[0])
    project(0)
    send_sides(R0, 0)
    send_sides(R0, 1)
    wait(got.at[1], enc_recv.at[1])
    project(1)
    send_sides(R1, 0)
    send_sides(R1, 1)
    for g in range(2):
        sent(R0, g)
        send_sides(L0, g)
        send_plane(R0, g)
    sent(R1, 0)
    sent(R1, 1)
    send_plane(R1, 0)
    send_plane(R1, 1)
    for g in range(2):
        sent(L0, g)
        send_sides(L1, g)

    wait(rights.at[core], right_recv)
    remote(rights.at[core], rights.at[core], twin_send, twin_recv, at(x * 2 + 1 - core, col, chan))
    send_plane(L0, 0)
    send_plane(L0, 1)
    place = lax.rem(y, 2) * 8 + x * 2 + y // 2

    def multiply():
        wait(rights.at[1 - core], twin_recv)
        wait(lefts, left_recv)

        def step(m, carry):
            n = lax.rem(m + z // 2, 4)
            parts = []
            for half in range(2):
                for yy in range(4):
                    for q in range(2):
                        start = pl.multiple_of((n * 2 + half) * 64 + yy * 16, 16)
                        parts.append(rights[q, pl.ds(start, 16), :])
            block = jnp.concatenate(parts, axis=0)
            result = lax.dot_general(
                lefts[...], block, (((1,), (1,)), ((), ())), preferred_element_type=jnp.float32
            )
            span = pl.ds(pl.multiple_of(n * 256, 256), 256)
            product[:, span] = result.astype(jnp.bfloat16)

            def go(t, carry):
                k = lax.rem(row * 4 + y + t, 32)
                remote(
                    product.at[pl.ds(pl.multiple_of(k * 16, 16), 16), span],
                    plane.at[core, place, :, span],
                    prod_send.at[n],
                    prod_recv.at[core * 2 + lax.rem(y, 2), n],
                    at(k // 4, col, lax.rem(k, 4) * 4 + zhi),
                )
                return carry

            lax.fori_loop(1, 32, go, 0)
            pltpu.make_async_copy(
                product.at[pl.ds(pl.multiple_of((row * 4 + y) * 16, 16), 16), span],
                plane.at[core, place, :, span],
                prod_recv.at[core * 2 + lax.rem(y, 2), n],
            ).start()
            return carry

        lax.fori_loop(0, 4, step, 0)

    def send_hidden(q, g):
        part = pl.ds(g * 8, 8)
        dst = hidden.at[q, pl.ds(pl.multiple_of(z * 16 + g * 8, 8), 8)]

        def go(m, carry):
            n = lax.rem(m + z // 2, 4)
            span = pl.ds(pl.multiple_of(n * 256, 256), 256)
            wait(plane.at[q, part, :, span], prod_recv.at[q * 2 + g, n])
            for half in range(2):
                block = n * 2 + half
                zz = lax.rem(block, 4) * 2 + block // 4
                src = plane.at[q, part, :, pl.ds(pl.multiple_of(block * 128, 128), 128)]

                @pl.when(zz == z)
                def _():
                    pltpu.make_async_copy(src, dst, hid_recv.at[q]).start()

                @pl.when(zz != z)
                def _():
                    remote(
                        src,
                        dst,
                        hid_send.at[q],
                        hid_recv.at[q],
                        at(row, lax.rem(zz, 2), y * 4 + zz // 2),
                    )

            return carry

        lax.fori_loop(0, 4, go, 0)

    @pl.when(core == 0)
    def _():
        multiply()

    send_plane(L1, 0)
    send_hidden(0, 0)
    send_plane(L1, 1)
    send_hidden(0, 1)

    @pl.when(core == 1)
    def _():
        multiply()

    send_hidden(1, 0)
    send_hidden(1, 1)

    def finish(q):
        wait(hidden.at[q], hid_recv.at[q])
        flat[...] = hidden[q].astype(jnp.float32).reshape(2048, 128)

        def step(i, carry):
            value = rows_of(flat, i)
            nu = jnp.sum(value, axis=0, keepdims=True) * (1.0 / 128)
            dev = value - nu
            tau = jnp.sum(dev * dev, axis=0, keepdims=True) * (1.0 / 128)
            short = value.astype(jnp.bfloat16)
            raw = jnp.dot(
                pieces[...],
                jnp.concatenate([short, short], axis=0),
                preferred_element_type=jnp.float32,
            )
            out_rows = (raw - twice(columns[2]) * nu) * lax.rsqrt(tau + EPS) + twice(columns[3])
            gated = jnp.concatenate([gate[q, 2 * i], gate[q, 2 * i + 1]], axis=1)
            put_rows(flat2, i, gated * out_rows)
            return carry

        lax.fori_loop(0, 8, step, 0)
        upd[q] = flat2[...].reshape(128, 16, 128).astype(jnp.bfloat16)
        dst = owned.at[
            :,
            pl.ds(pl.multiple_of(y * 32 + q * 16, 16), 16),
            pl.ds(pl.multiple_of(zhi * 128, 128), 128),
        ]

        def go(t, carry):
            p = lax.rem(chan + t, 16)
            remote(
                upd.at[q, pl.ds(pl.multiple_of(p * 8, 8), 8)],
                dst,
                upd_send.at[q],
                upd_recv,
                at(row, col, p),
            )
            return carry

        lax.fori_loop(1, 16, go, 0)
        pltpu.make_async_copy(
            upd.at[q, pl.ds(pl.multiple_of(chan * 8, 8), 8)], dst, upd_recv
        ).start()

    finish(0)
    finish(1)

    wait(enc.at[1, :15], enc_send.at[0])
    wait(plane.at[0, :14], hid_send.at[0])
    wait(plane.at[1, :14], hid_send.at[1])
    for q in range(2):
        wait(upd.at[q, :120], upd_send.at[q])
    for g in range(2):
        sent(L1, g)
    for s in range(4):

        @pl.when(core == s % 2)
        def _():
            wait(across.at[s, :15], plane_send.at[s])

        @pl.when(core != s % 2)
        def _():
            wait(across.at[s], plane_send.at[s])

    wait(rights.at[core], twin_send)
    for n in range(4):
        wait(product.at[:496, :256], prod_send.at[n])
    wait(owned, upd_recv)
    out[...] = owned[...]


def widen(narrow, wide):
    wide[...] = narrow[...].astype(jnp.float32)


def shards(
    pair,
    pair_mask,
    norm_gain,
    norm_bias,
    in_weight,
    gate_weight,
    hidden_gain,
    hidden_bias,
    out_weight,
):
    bf16, f32 = jnp.bfloat16, jnp.float32
    dma = pltpu.SemaphoreType.DMA
    vmem = pl.BlockSpec(memory_space=pltpu.VMEM)
    update = pl.pallas_call(
        kernel,
        out_shape=jax.ShapeDtypeStruct((8, 128, 512), bf16),
        in_specs=[pl.BlockSpec(memory_space=pltpu.HBM)] * 9,
        out_specs=vmem,
        scratch_shapes=[
            pltpu.VMEM((2, 4, 8, 16, 512), f32),
            pltpu.VMEM((32, 128), jnp.int32),
            pltpu.VMEM((1, 128), f32),
            pltpu.VMEM((1, 128), f32),
            pltpu.VMEM((128, 512), bf16),
            pltpu.VMEM((128, 128), bf16),
            pltpu.VMEM((1, 128), f32),
            pltpu.VMEM((1, 128), f32),
            pltpu.VMEM((128, 128), bf16),
            pltpu.VMEM((2, 16, 8, 16, 128), jnp.int16),
            pltpu.VMEM((2, 128, 16, 128), jnp.int16),
            pltpu.VMEM((2048, 128), f32),
            pltpu.VMEM((2048, 128), f32),
            pltpu.VMEM((32, 128), f32),
            pltpu.VMEM((4, 128, 128), f32),
            pltpu.VMEM((640, 128), bf16),
            pltpu.VMEM((128, 256), bf16),
            pltpu.VMEM((4, 128, 16, 128), bf16),
            pltpu.VMEM((4, 16, 16, 1024), bf16),
            pltpu.VMEM((2, 512, 1024), bf16),
            pltpu.VMEM((512, 1024), bf16),
            pltpu.VMEM((512, 1024), bf16),
            pltpu.VMEM((2, 16, 16, 1024), bf16),
            pltpu.VMEM((2, 128, 16, 128), bf16),
            pltpu.VMEM((2, 16, 128, 128), f32),
            pltpu.VMEM((2, 128, 16, 128), bf16),
            pltpu.VMEM((8, 128, 512), bf16),
            dma((2,)),
            dma((8,)),
            dma((16,)),
            dma((2,)),
            dma((4, 2)),
            dma((4, 2)),
            dma((4,)),
            dma,
            dma,
            dma,
            dma,
            dma((4,)),
            dma((4, 4)),
            dma((2,)),
            dma((2,)),
            dma((2,)),
            dma,
        ],
        compiler_params=pltpu.CompilerParams(
            collective_id=0, has_side_effects=True, vmem_limit_bytes=62 * 2**20
        ),
        name="triangle",
    )(
        pair,
        pair_mask,
        norm_gain.reshape(1, 128),
        norm_bias.reshape(1, 128),
        in_weight,
        gate_weight,
        hidden_gain.reshape(1, 128),
        hidden_bias.reshape(1, 128),
        out_weight,
    )
    block = pl.BlockSpec((4, 128, 512), lambda n: (n, 0, 0))
    return pl.pallas_call(
        widen,
        grid=(2,),
        out_shape=jax.ShapeDtypeStruct((8, 128, 512), f32),
        in_specs=[block],
        out_specs=block,
        name="widen",
    )(update)


def solution(mesh):
    placed = (P("chan", "row", "col"), P("row", "col"), P(), P(), P(), P(), P(), P(), P())
    return jax.shard_map(
        shards, mesh=mesh, in_specs=placed, out_specs=P("chan", "row", "col"), check_vma=False
    )
```
